32 devices in a mesh: edata: 4 (over x, core), expert: 8 (over z, y).
Axes of the slice: x: 2, y: 2, z: 4, core: 2. Of those that a mesh axis runs over, the one named last changes fastest.
Arguments:
- tokens_one: bfloat16 [512, 3584], P(('edata', 'expert')), may hold values from -6 to 6
- routes_one: int32 [512, 2], P(('edata', 'expert')), may hold values from 0 to 7, all different within a row; in each aligned block of 16 rows (0 to 15, 16 to 31, ...) at most 5 rows name the same one
- gates_one: float32 [512, 2], P(('edata', 'expert')), may hold values from 0.2 to 1
- tokens_two: bfloat16 [512, 3584], P(('edata', 'expert')), may hold values from -6 to 6
- routes_two: int32 [512, 2], P(('edata', 'expert')), may hold values from 0 to 7, all different within a row; in each aligned block of 16 rows (0 to 15, 16 to 31, ...) at most 5 rows name the same one
- gates_two: float32 [512, 2], P(('edata', 'expert')), may hold values from 0.2 to 1
- cot_two: bfloat16 [512, 3584], P(('edata', 'expert')), may hold values from -6 to 6
- rows_three: bfloat16 [1024, 3584], P(('edata', 'expert')), may hold values from -6 to 6
- cot_three: bfloat16 [1024, 3584], P(('edata', 'expert')), may hold values from -0.29882812 to 0.29882812
- w_gate: bfloat16 [3584, 1024], P(None, 'expert'), may hold values from -0.09375 to 0.09375
- w_up: bfloat16 [3584, 1024], P(None, 'expert'), may hold values from -0.09375 to 0.09375
- w_down: bfloat16 [1024, 3584], P('expert'), may hold values from -0.5 to 0.5
Outputs:
- out_one: bfloat16 [512, 3584], P(('edata', 'expert'))
- dx_two: bfloat16 [512, 3584], P(('edata', 'expert'))
- weight_grads: bfloat16 [3584, 3, 1024], P('edata', None, 'expert')
The draws below stay inside these ranges and needn't reach their ends.
Inputs may be any that keep to these rules, and one draw needn't show every extreme that they name: `routes_one`: each row names 2 different experts; among the rows of one device no expert is named more than 5 times, and that count is reached. `routes_two`: each row names 2 different experts; among the rows of one device no expert is named more than 5 times, and that count is reached.
All inputs are finite; a program needn't handle non-finite values.
Results may differ from the reference program's by a relative error of at most 0.009.
Values may be sent and summed in bfloat16 or wider, within the bound.
A program may use at most 64 MiB of HBM per device.

```python
import math
import jax
import jax.numpy as jnp
import numpy as np
from jax import lax

D = 3584
H_DEV = 128
EXPERTS = 8
TOP = 2
TOK_DEV = 16
W_ROWS = 32
SLICES = 1
HIDDEN_SIZE = 128
CAP = 5
TOKENS = 512
W_TOTAL = 1024
N_EDATA = 4
N_EXPERT = 8
DEVICES = 32


def with_spikes(drawn, rng, source, target, blocks, factor):
    def block_of(dim):
        return (jnp.arange(drawn.shape[dim]) // (drawn.shape[dim] // blocks)).reshape((-1,) + (1,) * (drawn.ndim - 1 - dim))

    near = jax.random.permutation(rng, blocks)[block_of(target)]
    far = (block_of(target) + blocks // 2) % blocks
    return jnp.where((block_of(source) == near) | (block_of(source) == far), factor * drawn, drawn)


def block_levels(key, shape, pieces, low, high):
    level = 1.0
    for axis_at, parts in pieces:
        draws = jax.random.uniform(jax.random.fold_in(jax.random.fold_in(key, 6), axis_at), (parts,), jnp.float32, low / len(pieces), high / len(pieces))
        level = level * jnp.repeat(jnp.exp(draws), shape[axis_at] // parts).reshape((-1,) + (1,) * (len(shape) - 1 - axis_at))
    return level


def shared_out(stream_key, own, number, rows, number_of, top, reach, slope):
    order = jax.random.permutation(stream_key, number_of)
    heavy_load, usual = portions_of(number_of, rows * top, reach, slope, True), portions_of(number_of, rows * top, reach, slope, False)
    places = jnp.arange(number_of)

    def named(lengths, offset_by):
        used = int((lengths > 0).sum())
        fixed = max(1, used // 4)
        passed = fixed + (places - fixed + offset_by * (used - fixed)) % max(1, number_of - fixed)
        return jnp.zeros((number_of,), jnp.int32).at[order[jnp.where(places < fixed, places, passed)]].set(jnp.asarray(lengths, jnp.int32))

    lengths = jnp.where(number % 4 == 0, named(heavy_load, number // 4), named(usual, number - number // 4 - 1))
    mixed = jax.random.permutation(jax.random.fold_in(own, 3), number_of)
    donor, sink = mixed[0:number_of // 2 * 2:2], mixed[1:number_of // 2 * 2:2]
    margin = jnp.minimum(lengths[donor] - 1, reach - lengths[sink]) // 2
    margin = jnp.where((donor == order[0]) | (sink == order[0]) | (lengths[sink] == 0), 0, jnp.maximum(margin, 0))
    passed = jax.random.randint(jax.random.fold_in(own, 4), (number_of // 2,), 0, 1 << 20) % (margin + 1)
    lengths = lengths.at[donor].add(-passed).at[sink].add(passed)
    labels = jnp.searchsorted(jnp.cumsum(lengths), jnp.arange(rows * top), side="right").astype(jnp.int32)
    table = labels.reshape(top, rows).T
    table = table[jax.random.permutation(jax.random.fold_in(own, 1), rows)]
    offset_by = jax.random.randint(jax.random.fold_in(own, 2), (rows, 1), 0, top)
    return jnp.take_along_axis(table, (jnp.arange(top)[None, :] + offset_by) % top, axis=1)


def portions_of(count, total, most, skew, full):
    weights = [(1 << 20) // math.isqrt(rank ** skew) + 1 for rank in range(1, count + 1)]
    largest = most if full else min(most, max(-(-total // count), total * weights[0] // sum(weights)))
    least = 1 if total - largest >= count - 1 else 0
    counts, spare = [largest] + [least] * (count - 1), total - largest - least * (count - 1)
    while spare > 0:
        candidates = [i for i in range(1, count) if counts[i] < largest] or [i for i in range(1, count) if counts[i] < most]
        pool, budget = sum([weights[i] for i in candidates]), spare
        for i in candidates:
            more = min(most - counts[i], max(1, budget * weights[i] // pool), spare)
            counts[i] = counts[i] + more
            spare = spare - more
    return np.array(counts)


def bell_draw(stream_key, dims, deviation, reach, split=(), held_as=jnp.bfloat16):
    values = deviation * jax.random.normal(stream_key, dims, jnp.float32)
    if split:
        values = values * block_levels(stream_key, dims, split, -0.22, 0.18)
    return jnp.clip(values, -reach, reach).astype(held_as)


def bell_draw_with(own_key, shape, spread, most, shards, heavy, kind=jnp.bfloat16):
    entries = spread * jax.random.normal(own_key, shape, jnp.float32)
    if shards:
        entries = entries * block_levels(own_key, shape, shards, -0.22, 0.18)
    return jnp.clip(with_spikes(entries, jax.random.fold_in(own_key, 3), *heavy), -most, most).astype(kind)


def setup_inputs(seed: int = 0) -> dict:
    keys = jax.random.split(jax.random.key(seed), 13)
    tokens_one = bell_draw(keys[0], (TOKENS, D), 1.0, 6.0, ((0, 32),))
    routes_one_keys = jax.random.split(jax.random.fold_in(keys[1], 1), TOKENS // TOK_DEV)
    routes_one_turns = jax.random.permutation(jax.random.fold_in(keys[1], 3), TOKENS // TOK_DEV)
    routes_one = jax.vmap(lambda own, number: shared_out(jax.random.fold_in(keys[1], 2), own, number, TOK_DEV, EXPERTS, TOP, CAP, 2))(routes_one_keys, routes_one_turns).reshape((TOKENS, TOP))
    gates_one = jnp.clip(0.2 + 0.8 * jax.random.uniform(keys[2], (TOKENS, TOP), jnp.float32) ** block_levels(keys[2], (TOKENS, TOP), ((0, 32),), -0.2, 0.2), 0.2, 1.0)
    tokens_two = bell_draw(keys[3], (TOKENS, D), 1.0, 6.0, ((0, 32),))
    routes_two_keys = jax.random.split(jax.random.fold_in(keys[4], 1), TOKENS // TOK_DEV)
    routes_two_turns = jax.random.permutation(jax.random.fold_in(keys[4], 3), TOKENS // TOK_DEV)
    routes_two = jax.vmap(lambda own, number: shared_out(jax.random.fold_in(keys[4], 2), own, number, TOK_DEV, EXPERTS, TOP, CAP, 2))(routes_two_keys, routes_two_turns).reshape((TOKENS, TOP))
    gates_two = jnp.clip(0.2 + 0.8 * jax.random.uniform(keys[5], (TOKENS, TOP), jnp.float32) ** block_levels(keys[5], (TOKENS, TOP), ((0, 32),), -0.2, 0.2), 0.2, 1.0)
    cot_two = bell_draw(keys[6], (TOKENS, D), 1.0, 6.0, ((0, 32),))
    rows_three = bell_draw_with(keys[7], (W_TOTAL, D), 1.0, 6.0, ((0, 32),), (0, 1, 32, 2.75))
    cot_three = bell_draw(keys[8], (W_TOTAL, D), 0.05, 0.29882812, ((0, 32),))
    w_gate = bell_draw(keys[9], (D, EXPERTS * HIDDEN_SIZE), D ** -0.5, 0.09375, ((1, 8),))
    w_up = bell_draw(keys[10], (D, EXPERTS * HIDDEN_SIZE), D ** -0.5, 0.09375, ((1, 8),))
    w_down = bell_draw(keys[11], (EXPERTS * HIDDEN_SIZE, D), HIDDEN_SIZE ** -0.5, 0.5, ((0, 8),))
    return {"tokens_one": tokens_one, "routes_one": routes_one, "gates_one": gates_one, "tokens_two": tokens_two, "routes_two": routes_two, "gates_two": gates_two, "cot_two": cot_two, "rows_three": rows_three, "cot_three": cot_three, "w_gate": w_gate, "w_up": w_up, "w_down": w_down}


def forward_factors(block_rows, slice_gate, slice_up):
    gate_pre = jnp.dot(block_rows, slice_gate, preferred_element_type=jnp.float32)
    up_pre = jnp.dot(block_rows, slice_up, preferred_element_type=jnp.float32)
    gate_sigma = jax.nn.sigmoid(gate_pre)
    hidden = (gate_pre * gate_sigma * up_pre).astype(jnp.bfloat16)
    return gate_pre, up_pre, gate_sigma, hidden


def backward_factors(block_cot, slice_down, gate_pre, up_pre, gate_sigma):
    d_hidden = lax.dot_general(block_cot, slice_down, (((1,), (1,)), ((), ())), preferred_element_type=jnp.float32)
    d_gate = (d_hidden * up_pre * gate_sigma * (1.0 + gate_pre * (1.0 - gate_sigma))).astype(jnp.bfloat16)
    d_up = (d_hidden * gate_pre * gate_sigma).astype(jnp.bfloat16)
    return d_gate, d_up


def transpose_product(factor, weights):
    return lax.dot_general(factor, weights, (((1,), (1,)), ((), ())), preferred_element_type=jnp.float32)


def column_product(matrix, factor):
    return lax.dot_general(matrix, factor, (((0,), (0,)), ((), ())), preferred_element_type=jnp.float32)


def route_tables(routes, gates):
    route_list = routes.reshape(-1).astype(jnp.int32)
    gate_list = gates.reshape(-1)
    expert_ids = jnp.arange(EXPERTS, dtype=jnp.int32)
    onehot = (route_list[:, None] == expert_ids[None, :]).astype(jnp.int32)
    position = jnp.sum((jnp.cumsum(onehot, axis=0) - onehot) * onehot, axis=1).astype(jnp.int32)
    owner_ids = (jnp.arange(route_list.shape[0], dtype=jnp.int32) // TOP).astype(jnp.int32)
    capacity = CAP * DEVICES
    token_table = jnp.full((EXPERTS, capacity), TOKENS, jnp.int32).at[route_list, position].set(owner_ids)
    gate_table = jnp.zeros((EXPERTS, capacity), jnp.float32).at[route_list, position].set(gate_list)
    return token_table, gate_table


def reference(tokens_one, routes_one, gates_one, tokens_two, routes_two, gates_two, cot_two, rows_three, cot_three, w_gate, w_up, w_down):
    slice_ids = jnp.arange(N_EXPERT, dtype=jnp.int32)

    def weights_of(slice_index):
        first_column = (slice_index * H_DEV).astype(jnp.int32)
        return (lax.dynamic_slice_in_dim(w_gate, first_column, H_DEV, 1),
                lax.dynamic_slice_in_dim(w_up, first_column, H_DEV, 1),
                lax.dynamic_slice_in_dim(w_down, first_column, H_DEV, 0))

    zero_row = jnp.zeros((1, D), jnp.bfloat16)
    padded_one = jnp.concatenate([tokens_one, zero_row], axis=0)
    table_one, weight_one = route_tables(routes_one, gates_one)

    def forward_step(running, slice_index):
        slice_gate, slice_up, slice_down = weights_of(slice_index)
        expert = slice_index // SLICES
        token_ids = table_one[expert]
        block_rows = padded_one[token_ids]
        gate_pre, up_pre, gate_sigma, hidden = forward_factors(block_rows, slice_gate, slice_up)
        partial_value = jnp.dot(hidden, slice_down, preferred_element_type=jnp.float32).astype(jnp.bfloat16)
        contribution = weight_one[expert][:, None] * partial_value.astype(jnp.float32)
        return running.at[token_ids].add(contribution), None

    total_one, _ = lax.scan(forward_step, jnp.zeros((TOKENS + 1, D), jnp.float32), slice_ids)
    out_one = total_one[:TOKENS].astype(jnp.bfloat16)

    padded_two = jnp.concatenate([tokens_two, zero_row], axis=0)
    padded_cot = jnp.concatenate([cot_two, zero_row], axis=0)
    table_two, weight_two = route_tables(routes_two, gates_two)

    def backward_step(running, slice_index):
        slice_gate, slice_up, slice_down = weights_of(slice_index)
        expert = slice_index // SLICES
        token_ids = table_two[expert]
        block_rows = padded_two[token_ids]
        block_cot = (weight_two[expert][:, None] * padded_cot[token_ids].astype(jnp.float32)).astype(jnp.bfloat16)
        gate_pre, up_pre, gate_sigma, hidden = forward_factors(block_rows, slice_gate, slice_up)
        d_gate, d_up = backward_factors(block_cot, slice_down, gate_pre, up_pre, gate_sigma)
        partial_value = (transpose_product(d_gate, slice_gate) + transpose_product(d_up, slice_up)).astype(jnp.bfloat16)
        return running.at[token_ids].add(partial_value.astype(jnp.float32)), None

    total_two, _ = lax.scan(backward_step, jnp.zeros((TOKENS + 1, D), jnp.float32), slice_ids)
    dx_two = total_two[:TOKENS].astype(jnp.bfloat16)

    grouped_rows = rows_three.reshape(N_EDATA, N_EXPERT, W_ROWS, D)
    grouped_cot = cot_three.reshape(N_EDATA, N_EXPERT, W_ROWS, D)

    def slice_gradient(slice_index):
        slice_gate, slice_up, slice_down = weights_of(slice_index)

        def replica_term(replica_pair):
            block_rows, block_cot = replica_pair
            gate_pre, up_pre, gate_sigma, hidden = forward_factors(block_rows, slice_gate, slice_up)
            d_gate, d_up = backward_factors(block_cot, slice_down, gate_pre, up_pre, gate_sigma)
            stacked = jnp.stack([column_product(block_rows, d_gate), column_product(block_rows, d_up), column_product(block_cot, hidden)], axis=1)
            return lax.optimization_barrier(stacked.astype(jnp.bfloat16)).astype(jnp.float32)

        replica_terms = lax.map(replica_term, (grouped_rows[:, slice_index], grouped_cot[:, slice_index]))
        return jnp.sum(replica_terms, axis=0).astype(jnp.bfloat16)

    slice_grads = lax.map(slice_gradient, slice_ids)
    weight_grads = jnp.transpose(slice_grads, (1, 2, 0, 3)).reshape(D, 3, N_EXPERT * H_DEV)
    return out_one, dx_two, weight_grads
```

```python
import functools

import jax
import jax.numpy as jnp
from jax import lax
from jax.experimental import pallas as pl
from jax.experimental.pallas import tpu as pltpu
from jax.sharding import PartitionSpec as P

EXPERTS = 8
CAP = 5
BLOCK = 16
FOLD = 3
GROUP = 8
BF16 = jnp.bfloat16
F32 = jnp.float32
MESH = pl.DeviceIdType.MESH


def mm(a, b):
    return jnp.dot(a, b, preferred_element_type=F32)


def mm_nt(a, b):
    return lax.dot_general(a, b, (((1,), (1,)), ((), ())), preferred_element_type=F32)


def mm_tn(a, b):
    return lax.dot_general(a, b, (((0,), (0,)), ((), ())), preferred_element_type=F32)


def slots(routes, width, slices):
    count = routes.shape[0]
    lane = lax.broadcasted_iota(jnp.int32, (count, width), 1)
    expert = lane // (BLOCK * slices)
    at = lane % BLOCK
    first = routes[:, 0:1] == expert
    second = routes[:, 1:2] == expert
    named = jnp.where(first | second, 1.0, 0.0).astype(BF16)
    row = lax.broadcasted_iota(jnp.int32, (count, count), 0)
    column = lax.broadcasted_iota(jnp.int32, (count, count), 1)
    before = jnp.where(column < row, 1.0, 0.0).astype(BF16)
    position = mm(before, named)
    here = (position == (at % CAP).astype(F32)) & (at < FOLD * CAP)
    return first & here, second & here, at // CAP


def ones(mask):
    return jnp.where(mask, 1.0, 0.0).astype(BF16)


def kernel(
    n, ne, tok1, rt1, gt1, tok2, rt2, gt2, cot2, rows3, cot3, wg_hbm, wu_hbm, wd_hbm,
    out1, dx2, grads,
    wgu, wd, stack, snd, rcv, ret_snd, ret_rcv, snd3, rcv3, fac_snd, fac_rcv,
    w_sem, own_sem, snd_sem, rcv_sem, ret_snd_sem, ret_rcv_sem, e_snd_sem, e_rcv_sem,
):
    depth = tok1.shape[1]
    h = wd.shape[1]
    chunk = wd.shape[2]
    slices = n // EXPERTS
    span = depth // ne
    spans = [(j * chunk, min(chunk, depth - j * chunk)) for j in range(FOLD)]
    me = lax.axis_index("expert")
    mine = lax.axis_index("edata")

    def expert_peer(k):
        return lax.rem(me + k, n)

    def edata_peer(k):
        return lax.rem(mine + k, ne)

    barrier = pltpu.get_barrier_semaphore()
    for k in range(1, n):
        pl.semaphore_signal(barrier, inc=1, device_id=(mine, expert_peer(k)), device_id_type=MESH)
    for k in range(1, ne):
        pl.semaphore_signal(barrier, inc=1, device_id=(edata_peer(k), me), device_id_type=MESH)

    loads = []
    for j, (at, size) in enumerate(spans):
        loads.append(pltpu.make_async_copy(
            wg_hbm.at[pl.ds(at, size), :], wgu.at[j, pl.ds(0, size), pl.ds(0, h)], w_sem.at[len(loads)]))
        loads.append(pltpu.make_async_copy(
            wu_hbm.at[pl.ds(at, size), :], wgu.at[j, pl.ds(0, size), pl.ds(h, h)], w_sem.at[len(loads)]))
        loads.append(pltpu.make_async_copy(
            wd_hbm.at[:, pl.ds(at, size)], wd.at[j, :, pl.ds(0, size)], w_sem.at[len(loads)]))
    for load in loads:
        load.start()
    for j, (at, size) in enumerate(spans):
        if size < chunk:
            wgu[j, size:, :] = jnp.zeros((chunk - size, 2 * h), BF16)
            wd[j, :, size:] = jnp.zeros((h, chunk - size), BF16)
            for k in range(2):
                base = (k * FOLD + j) * BLOCK
                stack[base:base + BLOCK, size:] = jnp.zeros((BLOCK, chunk - size), BF16)

    def send_copy(u, k):
        peer = expert_peer(k)
        return pltpu.make_async_remote_copy(
            src_ref=snd.at[u, peer // slices], dst_ref=rcv.at[u, me],
            send_sem=snd_sem.at[u, k], recv_sem=rcv_sem.at[u, k],
            device_id=(mine, peer), device_id_type=MESH)

    def own_copy(u):
        return pltpu.make_async_copy(snd.at[u, me // slices], rcv.at[u, me], own_sem.at[u])

    def ret_copy(u, k):
        peer = expert_peer(k)
        return pltpu.make_async_remote_copy(
            src_ref=ret_snd.at[u, peer], dst_ref=ret_rcv.at[u, me],
            send_sem=ret_snd_sem.at[u, k], recv_sem=ret_rcv_sem.at[u, k],
            device_id=(mine, peer), device_id_type=MESH)

    def own_ret(u):
        return pltpu.make_async_copy(ret_snd.at[u, me], ret_rcv.at[u, me], own_sem.at[3 + u])

    def rows_copy(k):
        peer = edata_peer(k)
        return pltpu.make_async_remote_copy(
            src_ref=snd3.at[peer], dst_ref=rcv3.at[mine],
            send_sem=e_snd_sem.at[0, k], recv_sem=e_rcv_sem.at[0, k],
            device_id=(peer, me), device_id_type=MESH)

    def factor_copy(k):
        return pltpu.make_async_remote_copy(
            src_ref=fac_snd, dst_ref=fac_rcv.at[mine],
            send_sem=e_snd_sem.at[1, k], recv_sem=e_rcv_sem.at[1, k],
            device_id=(edata_peer(k), me), device_id_type=MESH)

    own_rows = pltpu.make_async_copy(snd3.at[mine], rcv3.at[mine], own_sem.at[5])
    own_factors = pltpu.make_async_copy(fac_snd, fac_rcv.at[mine], own_sem.at[6])

    def pack(u, masks, values, chunk_of):
        chosen = []
        for i, (mask, value) in enumerate(zip(masks, values)):
            for j, (at, size) in enumerate(spans):
                base = (i * FOLD + j) * BLOCK
                stack[base:base + BLOCK, 0:size] = value(at, size)
                chosen.append(ones(mask & (chunk_of == j)))
        picked = jnp.concatenate(chosen, axis=0)
        packed = mm_tn(picked, stack[0:picked.shape[0], :]).astype(BF16)
        snd[u] = packed.reshape(EXPERTS, BLOCK, chunk)

    width = EXPERTS * BLOCK
    first_one, second_one, chunk_of = slots(rt1[...], width, 1)
    pack(0, [first_one | second_one], [lambda at, size: tok1[:, at:at + size]], chunk_of)

    pl.semaphore_wait(barrier, n + ne - 2)
    order = list(range(1, n))
    for k in order:
        send_copy(0, k).start()
    own_copy(0).start()

    first_two, second_two, _ = slots(rt2[...], width, 1)
    pack(1, [first_two | second_two], [lambda at, size: tok2[:, at:at + size]], chunk_of)
    for k in order:
        send_copy(1, k).start()
    own_copy(1).start()

    def scaled(k):
        return lambda at, size: (gt2[:, k:k + 1] * cot2[:, at:at + size].astype(F32)).astype(BF16)

    pack(2, [first_two, second_two], [scaled(0), scaled(1)], chunk_of)
    for k in order:
        send_copy(2, k).start()
    own_copy(2).start()

    count3 = rows3.shape[0]
    for j in range(ne):
        snd3[j, 0:count3, :] = rows3[:, j * span:(j + 1) * span]
        snd3[j, count3:2 * count3, :] = cot3[:, j * span:(j + 1) * span]
    for k in range(1, ne):
        rows_copy(k).start()
    own_rows.start()

    for load in loads:
        load.wait()

    def activations(gate_up):
        gate = gate_up[:, 0:h]
        up = gate_up[:, h:2 * h]
        return gate, up, jax.nn.sigmoid(gate)

    def cotangents(d_hidden, gate, up, sigma):
        d_gate = (d_hidden * up * sigma * (1.0 + gate * (1.0 - sigma))).astype(BF16)
        d_up = (d_hidden * gate * sigma).astype(BF16)
        return d_gate, d_up

    gate_up = jnp.zeros((count3, 2 * h), F32)
    d_hidden = jnp.zeros((count3, h), F32)
    for j, (at, size) in enumerate(spans):
        gate_up = gate_up + mm(rows3[:, at:at + size], wgu[j, 0:size, :])
        d_hidden = d_hidden + mm_nt(cot3[:, at:at + size], wd[j, :, 0:size])
    gate, up, sigma = activations(gate_up)
    d_gate, d_up = cotangents(d_hidden, gate, up, sigma)
    fac_snd[:, 0:h] = d_gate
    fac_snd[:, h:2 * h] = d_up
    fac_snd[:, 2 * h:3 * h] = (gate * sigma * up).astype(BF16)
    for k in range(1, ne):
        factor_copy(k).start()
    own_factors.start()

    rows = GROUP * BLOCK
    row = lax.broadcasted_iota(jnp.int32, (rows, rows), 0)
    column = lax.broadcasted_iota(jnp.int32, (rows, rows), 1)
    join = jnp.where(
        (row // BLOCK == column // BLOCK)
        & (row % BLOCK % CAP == column % BLOCK % CAP)
        & (row % BLOCK < FOLD * CAP)
        & (column % BLOCK < FOLD * CAP),
        1.0, 0.0)

    def chunk_mask(j, size):
        slot = lax.broadcasted_iota(jnp.int32, (rows, size), 0) % BLOCK
        return slot // CAP == j

    def joined(parts):
        total = jnp.zeros_like(parts[0])
        for j, part in enumerate(parts):
            total = total + jnp.where(chunk_mask(j, part.shape[1]), part, 0.0)
        return jnp.dot(join, total, precision=lax.Precision.HIGHEST, preferred_element_type=F32)

    def spread(value, j):
        return jnp.where(chunk_mask(j, value.shape[1]), value, 0.0).astype(BF16)

    def groups(body):
        if n == GROUP:
            body(0)
        else:
            pl.loop(0, n // GROUP)(lambda b: body(b * GROUP))

    def block(ref, u, b):
        return ref[u, pl.ds(b, GROUP)].reshape(rows, chunk)

    def forward(b):
        x = block(rcv, 0, b)
        gate, up, sigma = activations(joined([mm(x, wgu[j]) for j in range(FOLD)]))
        hidden = gate * sigma * up
        total = sum(mm(spread(hidden, j), wd[j]) for j in range(FOLD))
        ret_snd[0, pl.ds(b, GROUP)] = total.astype(BF16).reshape(GROUP, BLOCK, chunk)

    def backward(b):
        x = block(rcv, 1, b)
        y = block(rcv, 2, b)
        gate, up, sigma = activations(joined([mm(x, wgu[j]) for j in range(FOLD)]))
        d_hidden = joined([mm_nt(y, wd[j]) for j in range(FOLD)])
        d_gate, d_up = cotangents(d_hidden, gate, up, sigma)
        both = jnp.concatenate([d_gate.astype(F32), d_up.astype(F32)], axis=1)
        total = sum(mm_nt(spread(both, j), wgu[j]) for j in range(FOLD))
        ret_snd[1, pl.ds(b, GROUP)] = total.astype(BF16).reshape(GROUP, BLOCK, chunk)

    for k in order:
        send_copy(0, k).wait_recv()
    own_copy(0).wait()
    groups(forward)
    for k in order:
        ret_copy(0, k).start()
    own_ret(0).start()

    for k in range(1, ne):
        rows_copy(k).wait_recv()
        factor_copy(k).wait_recv()
    own_rows.wait()
    own_factors.wait()
    all_rows = rcv3[:, 0:count3, :].reshape(ne * count3, span)
    all_cots = rcv3[:, count3:2 * count3, :].reshape(ne * count3, span)
    factors = fac_rcv[...].reshape(ne * count3, 3 * h)
    pair = mm_tn(all_rows, factors[:, 0:2 * h]).astype(BF16)
    grads[0] = pair[:, 0:h]
    grads[1] = pair[:, h:2 * h]
    grads[2] = mm_tn(all_cots, factors[:, 2 * h:3 * h]).astype(BF16)

    for u in (1, 2):
        for k in order:
            send_copy(u, k).wait_recv()
        own_copy(u).wait()
    groups(backward)
    for k in order:
        ret_copy(1, k).start()
    own_ret(1).start()

    back = n * BLOCK

    for k in order:
        ret_copy(0, k).wait_recv()
    own_ret(0).wait()
    first, second, back_chunk = slots(rt1[...], back, slices)
    weight = jnp.where(first, gt1[:, 0:1], 0.0) + jnp.where(second, gt1[:, 1:2], 0.0)
    high = weight.astype(BF16)
    rest = weight - high.astype(F32)
    middle = rest.astype(BF16)
    low = (rest - middle.astype(F32)).astype(BF16)
    answer = ret_rcv[0].reshape(back, chunk)
    for j, (at, size) in enumerate(spans):
        select = jnp.where(back_chunk == j, 1.0, 0.0)
        pieces = jnp.concatenate(
            [(piece.astype(F32) * select).astype(BF16) for piece in (high, middle, low)], axis=0)
        result = mm(pieces, answer[:, 0:size])
        out1[:, at:at + size] = (
            result[0:BLOCK] + result[BLOCK:2 * BLOCK] + result[2 * BLOCK:3 * BLOCK]).astype(BF16)

    for k in order:
        ret_copy(1, k).wait_recv()
    own_ret(1).wait()
    first, second, back_chunk = slots(rt2[...], back, slices)
    answer = ret_rcv[1].reshape(back, chunk)
    for j, (at, size) in enumerate(spans):
        picked = ones((first | second) & (back_chunk == j))
        dx2[:, at:at + size] = mm(picked, answer[:, 0:size]).astype(BF16)

    for k in order:
        for u in range(3):
            send_copy(u, k).wait_send()
        for u in range(2):
            ret_copy(u, k).wait_send()
    for k in range(1, ne):
        rows_copy(k).wait_send()
        factor_copy(k).wait_send()


def shards(*args):
    n = lax.axis_size("expert")
    ne = lax.axis_size("edata")
    tokens, depth = args[0].shape
    count3 = args[7].shape[0]
    h = args[9].shape[1]
    span = depth // ne
    chunk = -(-depth // (FOLD * 128)) * 128
    vmem = pl.BlockSpec(memory_space=pltpu.VMEM)
    hbm = pl.BlockSpec(memory_space=pl.ANY)
    out_one, dx_two, grads = pl.pallas_call(
        functools.partial(kernel, n, ne),
        out_shape=(
            jax.ShapeDtypeStruct((tokens, depth), BF16),
            jax.ShapeDtypeStruct((tokens, depth), BF16),
            jax.ShapeDtypeStruct((3, span, h), BF16),
        ),
        in_specs=[vmem] * 9 + [hbm] * 3,
        out_specs=(vmem, vmem, vmem),
        scratch_shapes=[
            pltpu.VMEM((FOLD, chunk, 2 * h), BF16),
            pltpu.VMEM((FOLD, h, chunk), BF16),
            pltpu.VMEM((2 * FOLD * BLOCK, chunk), BF16),
            pltpu.VMEM((3, EXPERTS, BLOCK, chunk), BF16),
            pltpu.VMEM((3, n, BLOCK, chunk), BF16),
            pltpu.VMEM((2, n, BLOCK, chunk), BF16),
            pltpu.VMEM((2, n, BLOCK, chunk), BF16),
            pltpu.VMEM((ne, 2 * count3, span), BF16),
            pltpu.VMEM((ne, 2 * count3, span), BF16),
            pltpu.VMEM((count3, 3 * h), BF16),
            pltpu.VMEM((ne, count3, 3 * h), BF16),
            pltpu.SemaphoreType.DMA((3 * FOLD,)),
            pltpu.SemaphoreType.DMA((7,)),
            pltpu.SemaphoreType.DMA((3, n)),
            pltpu.SemaphoreType.DMA((3, n)),
            pltpu.SemaphoreType.DMA((2, n)),
            pltpu.SemaphoreType.DMA((2, n)),
            pltpu.SemaphoreType.DMA((2, ne)),
            pltpu.SemaphoreType.DMA((2, ne)),
        ],
        compiler_params=pltpu.CompilerParams(
            collective_id=0, has_side_effects=True, vmem_limit_bytes=48 * 2**20),
    )(*args)
    return out_one, dx_two, jnp.transpose(grads, (1, 0, 2))


def solution(mesh):
    both = P(("edata", "expert"), None)
    return jax.shard_map(
        shards,
        mesh=mesh,
        in_specs=(both,) * 9 + (P(None, "expert"), P(None, "expert"), P("expert", None)),
        out_specs=(both, both, P("edata", None, "expert")),
        check_vma=False,
    )
```

```python
import functools

import jax
import jax.numpy as jnp
from jax import lax
from jax.experimental import pallas as pl
from jax.experimental.pallas import tpu as pltpu
from jax.sharding import PartitionSpec as P

EXPERTS = 8
CAP = 5
BLOCK = 16
FOLD = 3
GROUP = 8
BF16 = jnp.bfloat16
F32 = jnp.float32
MESH = pl.DeviceIdType.MESH


def mm(a, b):
    return jnp.dot(a, b, preferred_element_type=F32)


def mm_nt(a, b):
    return lax.dot_general(a, b, (((1,), (1,)), ((), ())), preferred_element_type=F32)


def mm_tn(a, b):
    return lax.dot_general(a, b, (((0,), (0,)), ((), ())), preferred_element_type=F32)


def slots(routes, width, slices):
    count = routes.shape[1]
    row = lax.broadcasted_iota(jnp.int32, (width, count), 0)
    expert = row // (BLOCK * slices)
    at = row % BLOCK
    first = routes[0:1, :] == expert
    second = routes[1:2, :] == expert
    named = jnp.where(first | second, 1.0, 0.0).astype(BF16)
    earlier = lax.broadcasted_iota(jnp.int32, (count, count), 0)
    later = lax.broadcasted_iota(jnp.int32, (count, count), 1)
    before = jnp.where(earlier < later, 1.0, 0.0).astype(BF16)
    position = mm(named, before)
    here = (position == (at % CAP).astype(F32)) & (at < FOLD * CAP)
    return first & here, second & here, at // CAP


def turned(piece):
    count = piece.shape[1]
    row = lax.broadcasted_iota(jnp.int32, (count, count), 0)
    column = lax.broadcasted_iota(jnp.int32, (count, count), 1)
    return mm_nt(jnp.where(row == column, 1.0, 0.0).astype(BF16), piece).astype(BF16)


def ones(mask):
    return jnp.where(mask, 1.0, 0.0).astype(BF16)


def kernel(
    n, ne, tok1_hbm, rt1_hbm, gt1_hbm, tok2_hbm, rt2_hbm, gt2_hbm, cot2_hbm, rows3_hbm, cot3_hbm,
    wg_hbm, wu_hbm, wd_hbm,
    out1, dx2, grads,
    tok1, rt1, gt1, tok2, rt2, gt2, cot2, rows3, cot3, in_sem,
    wgu, wd, stack, snd, rcv, ret_snd, ret_rcv, snd3, rcv3, fac_snd, fac_rcv,
    w_sem, own_sem, snd_sem, rcv_sem, ret_snd_sem, ret_rcv_sem, e_snd_sem, e_rcv_sem,
):
    depth = tok1.shape[1]
    h = wd.shape[1]
    chunk = wd.shape[2]
    slices = n // EXPERTS
    span = depth // ne
    spans = [(j * chunk, min(chunk, depth - j * chunk)) for j in range(FOLD)]
    me = lax.axis_index("expert")
    mine = lax.axis_index("edata")

    def expert_peer(k):
        return lax.rem(me + k, n)

    def edata_peer(k):
        return lax.rem(mine + k, ne)

    barrier = pltpu.get_barrier_semaphore()
    for k in range(1, n):
        pl.semaphore_signal(barrier, inc=1, device_id=(mine, expert_peer(k)), device_id_type=MESH)
    for k in range(1, ne):
        pl.semaphore_signal(barrier, inc=1, device_id=(edata_peer(k), me), device_id_type=MESH)

    pairs = (
        (rt1_hbm, rt1), (tok1_hbm, tok1), (rt2_hbm, rt2), (tok2_hbm, tok2), (gt2_hbm, gt2),
        (cot2_hbm, cot2), (gt1_hbm, gt1), (rows3_hbm, rows3), (cot3_hbm, cot3))
    inputs = [pltpu.make_async_copy(a, b, in_sem.at[i]) for i, (a, b) in enumerate(pairs)]
    for load in inputs:
        load.start()
    loads = []
    for j, (at, size) in enumerate(spans):
        loads.append(pltpu.make_async_copy(
            wg_hbm.at[pl.ds(at, size), :], wgu.at[j, pl.ds(0, size), pl.ds(0, h)], w_sem.at[len(loads)]))
        loads.append(pltpu.make_async_copy(
            wu_hbm.at[pl.ds(at, size), :], wgu.at[j, pl.ds(0, size), pl.ds(h, h)], w_sem.at[len(loads)]))
        loads.append(pltpu.make_async_copy(
            wd_hbm.at[:, pl.ds(at, size)], wd.at[j, :, pl.ds(0, size)], w_sem.at[len(loads)]))
    for load in loads:
        load.start()
    for j, (at, size) in enumerate(spans):
        if size < chunk:
            wgu[j, size:, :] = jnp.zeros((chunk - size, 2 * h), BF16)
            wd[j, :, size:] = jnp.zeros((h, chunk - size), BF16)
            stack[j * BLOCK:(j + 1) * BLOCK, size:] = jnp.zeros((BLOCK, chunk - size), BF16)

    def send_copy(u, k):
        peer = expert_peer(k)
        return pltpu.make_async_remote_copy(
            src_ref=snd.at[u, peer // slices], dst_ref=rcv.at[u, me],
            send_sem=snd_sem.at[u, k], recv_sem=rcv_sem.at[u, k],
            device_id=(mine, peer), device_id_type=MESH)

    def own_copy(u):
        return pltpu.make_async_copy(snd.at[u, me // slices], rcv.at[u, me], own_sem.at[u])

    def ret_copy(u, k):
        peer = expert_peer(k)
        return pltpu.make_async_remote_copy(
            src_ref=ret_snd.at[u, peer], dst_ref=ret_rcv.at[u, me],
            send_sem=ret_snd_sem.at[u, k], recv_sem=ret_rcv_sem.at[u, k],
            device_id=(mine, peer), device_id_type=MESH)

    def own_ret(u):
        return pltpu.make_async_copy(ret_snd.at[u, me], ret_rcv.at[u, me], own_sem.at[3 + u])

    def rows_copy(k):
        peer = edata_peer(k)
        return pltpu.make_async_remote_copy(
            src_ref=snd3.at[peer], dst_ref=rcv3.at[mine],
            send_sem=e_snd_sem.at[0, k], recv_sem=e_rcv_sem.at[0, k],
            device_id=(peer, me), device_id_type=MESH)

    def factor_copy(k):
        return pltpu.make_async_remote_copy(
            src_ref=fac_snd, dst_ref=fac_rcv.at[mine],
            send_sem=e_snd_sem.at[1, k], recv_sem=e_rcv_sem.at[1, k],
            device_id=(edata_peer(k), me), device_id_type=MESH)

    own_rows = pltpu.make_async_copy(snd3.at[mine], rcv3.at[mine], own_sem.at[5])
    own_factors = pltpu.make_async_copy(fac_snd, fac_rcv.at[mine], own_sem.at[6])

    def pack(u, mask, source, scale):
        for j, (at, size) in enumerate(spans):
            stack[j * BLOCK:(j + 1) * BLOCK, 0:size] = source[:, at:at + size]
        total = jnp.zeros((width, chunk), F32)
        for j in range(FOLD):
            total = total + mm(ones(mask & (chunk_of == j)), stack[j * BLOCK:(j + 1) * BLOCK, :])
        if scale is not None:
            total = total * scale
        snd[u] = total.astype(BF16).reshape(EXPERTS, BLOCK, chunk)

    width = EXPERTS * BLOCK
    inputs[0].wait()
    first_one, second_one, chunk_of = slots(rt1[...], width, 1)
    inputs[1].wait()
    pack(0, first_one | second_one, tok1, None)

    pl.semaphore_wait(barrier, n + ne - 2)
    order = list(range(1, n))
    for k in order:
        send_copy(0, k).start()
    own_copy(0).start()

    for load in inputs[2:]:
        load.wait()
    first_two, second_two, _ = slots(rt2[...], width, 1)
    pack(1, first_two | second_two, tok2, None)
    for k in order:
        send_copy(1, k).start()
    own_copy(1).start()

    scale = (
        jnp.where(first_two, gt2[0:1, :], 0.0) + jnp.where(second_two, gt2[1:2, :], 0.0)
    ).sum(axis=1, keepdims=True)
    pack(2, first_two | second_two, cot2, scale)
    for k in order:
        send_copy(2, k).start()
    own_copy(2).start()

    count3 = rows3.shape[0]
    for j in range(ne):
        snd3[j, 0:count3, :] = rows3[:, j * span:(j + 1) * span]
        snd3[j, count3:2 * count3, :] = cot3[:, j * span:(j + 1) * span]
    for k in range(1, ne):
        rows_copy(k).start()
    own_rows.start()

    for load in loads:
        load.wait()

    def activations(gate_up):
        gate = gate_up[:, 0:h]
        up = gate_up[:, h:2 * h]
        return gate, up, jax.nn.sigmoid(gate)

    def cotangents(d_hidden, gate, up, sigma):
        d_gate = (d_hidden * up * sigma * (1.0 + gate * (1.0 - sigma))).astype(BF16)
        d_up = (d_hidden * gate * sigma).astype(BF16)
        return d_gate, d_up

    gate_up = jnp.zeros((count3, 2 * h), F32)
    d_hidden = jnp.zeros((count3, h), F32)
    for j, (at, size) in enumerate(spans):
        gate_up = gate_up + mm(rows3[:, at:at + size], wgu[j, 0:size, :])
        d_hidden = d_hidden + mm_nt(cot3[:, at:at + size], wd[j, :, 0:size])
    gate, up, sigma = activations(gate_up)
    d_gate, d_up = cotangents(d_hidden, gate, up, sigma)
    fac_snd[:, 0:h] = d_gate
    fac_snd[:, h:2 * h] = d_up
    fac_snd[:, 2 * h:3 * h] = (gate * sigma * up).astype(BF16)
    for k in range(1, ne):
        factor_copy(k).start()
    own_factors.start()

    rows = GROUP * BLOCK
    row = lax.broadcasted_iota(jnp.int32, (rows, rows), 0)
    column = lax.broadcasted_iota(jnp.int32, (rows, rows), 1)
    join = jnp.where(
        (row // BLOCK == column // BLOCK)
        & (row % BLOCK % CAP == column % BLOCK % CAP)
        & (row % BLOCK < FOLD * CAP)
        & (column % BLOCK < FOLD * CAP),
        1.0, 0.0)

    def chunk_mask(j, size):
        slot = lax.broadcasted_iota(jnp.int32, (rows, size), 0) % BLOCK
        return slot // CAP == j

    def joined(parts):
        total = jnp.zeros_like(parts[0])
        for j, part in enumerate(parts):
            total = total + jnp.where(chunk_mask(j, part.shape[1]), part, 0.0)
        return jnp.dot(join, total, precision=lax.Precision.HIGHEST, preferred_element_type=F32)

    def spread(value, j):
        return jnp.where(chunk_mask(j, value.shape[1]), value, 0.0).astype(BF16)

    def groups(body):
        if n == GROUP:
            body(0)
        else:
            pl.loop(0, n // GROUP)(lambda b: body(b * GROUP))

    def block(ref, u, b):
        return ref[u, pl.ds(b, GROUP)].reshape(rows, chunk)

    def forward(b):
        x = block(rcv, 0, b)
        gate, up, sigma = activations(joined([mm(x, wgu[j]) for j in range(FOLD)]))
        hidden = gate * sigma * up
        total = sum(mm(spread(hidden, j), wd[j]) for j in range(FOLD))
        ret_snd[0, pl.ds(b, GROUP)] = total.astype(BF16).reshape(GROUP, BLOCK, chunk)

    def backward(b):
        x = block(rcv, 1, b)
        y = block(rcv, 2, b)
        gate, up, sigma = activations(joined([mm(x, wgu[j]) for j in range(FOLD)]))
        d_hidden = joined([mm_nt(y, wd[j]) for j in range(FOLD)])
        d_gate, d_up = cotangents(d_hidden, gate, up, sigma)
        both = jnp.concatenate([d_gate.astype(F32), d_up.astype(F32)], axis=1)
        total = sum(mm_nt(spread(both, j), wgu[j]) for j in range(FOLD))
        ret_snd[1, pl.ds(b, GROUP)] = total.astype(BF16).reshape(GROUP, BLOCK, chunk)

    for k in order:
        send_copy(0, k).wait_recv()
    own_copy(0).wait()
    groups(forward)
    for k in order:
        ret_copy(0, k).start()
    own_ret(0).start()

    for k in range(1, ne):
        rows_copy(k).wait_recv()
        factor_copy(k).wait_recv()
    own_rows.wait()
    own_factors.wait()
    all_rows = rcv3[:, 0:count3, :].reshape(ne * count3, span)
    all_cots = rcv3[:, count3:2 * count3, :].reshape(ne * count3, span)
    factors = fac_rcv[...].reshape(ne * count3, 3 * h)
    pair = mm_tn(all_rows, factors[:, 0:2 * h]).astype(BF16)
    grads[0] = pair[:, 0:h]
    grads[1] = pair[:, h:2 * h]
    grads[2] = mm_tn(all_cots, factors[:, 2 * h:3 * h]).astype(BF16)

    for u in (1, 2):
        for k in order:
            send_copy(u, k).wait_recv()
        own_copy(u).wait()
    groups(backward)
    for k in order:
        ret_copy(1, k).start()
    own_ret(1).start()

    back = n * BLOCK
    first, second, back_chunk = slots(rt1[...], back, slices)
    weight = jnp.where(first, gt1[0:1, :], 0.0) + jnp.where(second, gt1[1:2, :], 0.0)
    pieces = []
    for j in range(FOLD):
        rest = jnp.where(back_chunk == j, weight, 0.0)
        split = []
        for _ in range(3):
            split.append(rest.astype(BF16))
            rest = rest - split[-1].astype(F32)
        pieces.append(jnp.concatenate([turned(piece) for piece in split], axis=0))
    first, second, back_chunk = slots(rt2[...], back, slices)
    picked = [turned(ones((first | second) & (back_chunk == j))) for j in range(FOLD)]

    for k in order:
        ret_copy(0, k).wait_recv()
    own_ret(0).wait()
    answer = ret_rcv[0].reshape(back, chunk)
    for j, (at, size) in enumerate(spans):
        result = mm(pieces[j], answer[:, 0:size])
        out1[:, at:at + size] = (
            result[0:BLOCK] + result[BLOCK:2 * BLOCK] + result[2 * BLOCK:3 * BLOCK]).astype(BF16)

    for k in order:
        ret_copy(1, k).wait_recv()
    own_ret(1).wait()
    answer = ret_rcv[1].reshape(back, chunk)
    for j, (at, size) in enumerate(spans):
        dx2[:, at:at + size] = mm(picked[j], answer[:, 0:size]).astype(BF16)

    for k in order:
        for u in range(3):
            send_copy(u, k).wait_send()
        for u in range(2):
            ret_copy(u, k).wait_send()
    for k in range(1, ne):
        rows_copy(k).wait_send()
        factor_copy(k).wait_send()


def store(a, b, c, a_out, b_out, c_out, sem):
    copies = [
        pltpu.make_async_copy(source, target, sem.at[i])
        for i, (source, target) in enumerate(((a, a_out), (b, b_out), (c, c_out)))]
    for copy in copies:
        copy.start()
    for copy in copies:
        copy.wait()


def shards(*args):
    args = [arg.T if i in (1, 2, 4, 5) else arg for i, arg in enumerate(args)]
    n = lax.axis_size("expert")
    ne = lax.axis_size("edata")
    tokens, depth = args[0].shape
    count3 = args[7].shape[0]
    h = args[9].shape[1]
    span = depth // ne
    chunk = -(-depth // (FOLD * 128)) * 128
    vmem = pl.BlockSpec(memory_space=pltpu.VMEM)
    hbm = pl.BlockSpec(memory_space=pl.ANY)
    results = (
            jax.ShapeDtypeStruct((tokens, depth), BF16),
            jax.ShapeDtypeStruct((tokens, depth), BF16),
            jax.ShapeDtypeStruct((3, span, h), BF16),
    )
    landed = pl.pallas_call(
        functools.partial(kernel, n, ne),
        out_shape=results,
        in_specs=[hbm] * 12,
        out_specs=(vmem, vmem, vmem),
        scratch_shapes=[pltpu.VMEM(arg.shape, arg.dtype) for arg in args[:9]] + [
            pltpu.SemaphoreType.DMA((9,)),
            pltpu.VMEM((FOLD, chunk, 2 * h), BF16),
            pltpu.VMEM((FOLD, h, chunk), BF16),
            pltpu.VMEM((FOLD * BLOCK, chunk), BF16),
            pltpu.VMEM((3, EXPERTS, BLOCK, chunk), BF16),
            pltpu.VMEM((3, n, BLOCK, chunk), BF16),
            pltpu.VMEM((2, n, BLOCK, chunk), BF16),
            pltpu.VMEM((2, n, BLOCK, chunk), BF16),
            pltpu.VMEM((ne, 2 * count3, span), BF16),
            pltpu.VMEM((ne, 2 * count3, span), BF16),
            pltpu.VMEM((count3, 3 * h), BF16),
            pltpu.VMEM((ne, count3, 3 * h), BF16),
            pltpu.SemaphoreType.DMA((3 * FOLD,)),
            pltpu.SemaphoreType.DMA((7,)),
            pltpu.SemaphoreType.DMA((3, n)),
            pltpu.SemaphoreType.DMA((3, n)),
            pltpu.SemaphoreType.DMA((2, n)),
            pltpu.SemaphoreType.DMA((2, n)),
            pltpu.SemaphoreType.DMA((2, ne)),
            pltpu.SemaphoreType.DMA((2, ne)),
        ],
        compiler_params=pltpu.CompilerParams(
            collective_id=0, has_side_effects=True, vmem_limit_bytes=62 * 2**20),
    )(*args)
    out_one, dx_two, grads = pl.pallas_call(
        store,
        out_shape=results,
        in_specs=[vmem] * 3,
        out_specs=(hbm,) * 3,
        scratch_shapes=[pltpu.SemaphoreType.DMA((3,))],
    )(*landed)
    return out_one, dx_two, jnp.transpose(grads, (1, 0, 2))


def solution(mesh):
    both = P(("edata", "expert"), None)
    return jax.shard_map(
        shards,
        mesh=mesh,
        in_specs=(both,) * 9 + (P(None, "expert"), P(None, "expert"), P("expert", None)),
        out_specs=(both, both, P("edata", None, "expert")),
        check_vma=False,
    )
```

```python
import functools

import jax
import jax.numpy as jnp
from jax import lax
from jax.experimental import pallas as pl
from jax.experimental.pallas import tpu as pltpu
from jax.sharding import PartitionSpec as P

EXPERTS = 8
CAP = 5
BLOCK = 16
FOLD = 3
GROUP = 8
BF16 = jnp.bfloat16
F32 = jnp.float32
MESH = pl.DeviceIdType.MESH


def mm(a, b):
    return jnp.dot(a, b, preferred_element_type=F32)


def mm_nt(a, b):
    return lax.dot_general(a, b, (((1,), (1,)), ((), ())), preferred_element_type=F32)


def mm_tn(a, b):
    return lax.dot_general(a, b, (((0,), (0,)), ((), ())), preferred_element_type=F32)


def slots(routes, width, slices):
    count = routes.shape[1]
    row = lax.broadcasted_iota(jnp.int32, (width, count), 0)
    expert = row // (BLOCK * slices)
    at = row % BLOCK
    first = routes[0:1, :] == expert
    second = routes[1:2, :] == expert
    named = jnp.where(first | second, 1.0, 0.0).astype(BF16)
    earlier = lax.broadcasted_iota(jnp.int32, (count, count), 0)
    later = lax.broadcasted_iota(jnp.int32, (count, count), 1)
    before = jnp.where(earlier < later, 1.0, 0.0).astype(BF16)
    position = mm(named, before)
    here = position == (at % CAP).astype(F32)
    pieces = [here & (at // CAP == j) for j in range(FOLD)]
    pieces += [(position == float(c)) & (at == FOLD * CAP) for c in range(CAP)]
    return first, second, pieces


def turned(piece):
    count = piece.shape[1]
    row = lax.broadcasted_iota(jnp.int32, (count, count), 0)
    column = lax.broadcasted_iota(jnp.int32, (count, count), 1)
    return mm_nt(jnp.where(row == column, 1.0, 0.0).astype(BF16), piece).astype(BF16)


def ones(mask):
    return jnp.where(mask, 1.0, 0.0).astype(BF16)


def kernel(
    n, ne, tok1_hbm, rt1_hbm, gt1_hbm, tok2_hbm, rt2_hbm, gt2_hbm, cot2_hbm, rows3_hbm, cot3_hbm,
    wg_hbm, wu_hbm, wd_hbm,
    out1, dx2, grads,
    tok1, rt1, gt1, tok2, rt2, gt2, cot2, rows3, cot3, in_sem,
    out1_buf, dx2_buf, grads_buf, out_sem, wgu_tail, wd_tail,
    wgu, wd, snd, rcv, ret_snd, ret_rcv, snd3, rcv3, fac_snd, fac_rcv,
    w_sem, own_sem, snd_sem, rcv_sem, ret_snd_sem, ret_rcv_sem, e_snd_sem, e_rcv_sem,
):
    depth = tok1.shape[1]
    h = wd.shape[1]
    chunk = wd.shape[2]
    slices = n // EXPERTS
    span = depth // ne
    spans = [(j * chunk, chunk) for j in range(FOLD)]
    cut = FOLD * chunk
    tail = depth - cut
    me = lax.axis_index("expert")
    mine = lax.axis_index("edata")

    def expert_peer(k):
        return lax.rem(me + k, n)

    def edata_peer(k):
        return lax.rem(mine + k, ne)

    barrier = pltpu.get_barrier_semaphore()
    for k in range(1, n):
        pl.semaphore_signal(barrier, inc=1, device_id=(mine, expert_peer(k)), device_id_type=MESH)
    for k in range(1, ne):
        pl.semaphore_signal(barrier, inc=1, device_id=(edata_peer(k), me), device_id_type=MESH)

    pairs = (
        (rt1_hbm, rt1), (tok1_hbm, tok1), (rt2_hbm, rt2), (tok2_hbm, tok2), (gt2_hbm, gt2),
        (cot2_hbm, cot2), (gt1_hbm, gt1), (rows3_hbm, rows3), (cot3_hbm, cot3))
    inputs = [pltpu.make_async_copy(a, b, in_sem.at[i]) for i, (a, b) in enumerate(pairs)]
    for load in inputs:
        load.start()
    loads = []
    for j, (at, size) in enumerate(spans):
        loads.append(pltpu.make_async_copy(
            wg_hbm.at[pl.ds(at, size), :], wgu.at[j, pl.ds(0, size), pl.ds(0, h)], w_sem.at[len(loads)]))
        loads.append(pltpu.make_async_copy(
            wu_hbm.at[pl.ds(at, size), :], wgu.at[j, pl.ds(0, size), pl.ds(h, h)], w_sem.at[len(loads)]))
        loads.append(pltpu.make_async_copy(
            wd_hbm.at[:, pl.ds(at, size)], wd.at[j, :, pl.ds(0, size)], w_sem.at[len(loads)]))
    for source, target in (
        (wg_hbm.at[pl.ds(cut, tail), :], wgu_tail.at[:, pl.ds(0, h)]),
        (wu_hbm.at[pl.ds(cut, tail), :], wgu_tail.at[:, pl.ds(h, h)]),
        (wd_hbm.at[:, pl.ds(cut, tail)], wd_tail),
    ):
        loads.append(pltpu.make_async_copy(source, target, w_sem.at[len(loads)]))
    for load in loads:
        load.start()
    def send_copy(u, k):
        peer = expert_peer(k)
        return pltpu.make_async_remote_copy(
            src_ref=snd.at[u, peer // slices], dst_ref=rcv.at[u, me],
            send_sem=snd_sem.at[u, k], recv_sem=rcv_sem.at[u, k],
            device_id=(mine, peer), device_id_type=MESH)

    def own_copy(u):
        return pltpu.make_async_copy(snd.at[u, me // slices], rcv.at[u, me], own_sem.at[u])

    def ret_copy(u, k):
        peer = expert_peer(k)
        return pltpu.make_async_remote_copy(
            src_ref=ret_snd.at[u, peer], dst_ref=ret_rcv.at[u, me],
            send_sem=ret_snd_sem.at[u, k], recv_sem=ret_rcv_sem.at[u, k],
            device_id=(mine, peer), device_id_type=MESH)

    def own_ret(u):
        return pltpu.make_async_copy(ret_snd.at[u, me], ret_rcv.at[u, me], own_sem.at[3 + u])

    def rows_copy(k):
        peer = edata_peer(k)
        return pltpu.make_async_remote_copy(
            src_ref=snd3.at[peer], dst_ref=rcv3.at[mine],
            send_sem=e_snd_sem.at[0, k], recv_sem=e_rcv_sem.at[0, k],
            device_id=(peer, me), device_id_type=MESH)

    def factor_copy(k):
        return pltpu.make_async_remote_copy(
            src_ref=fac_snd, dst_ref=fac_rcv.at[mine],
            send_sem=e_snd_sem.at[1, k], recv_sem=e_rcv_sem.at[1, k],
            device_id=(edata_peer(k), me), device_id_type=MESH)

    own_rows = pltpu.make_async_copy(snd3.at[mine], rcv3.at[mine], own_sem.at[5])
    own_factors = pltpu.make_async_copy(fac_snd, fac_rcv.at[mine], own_sem.at[6])

    def with_tails(total, tails):
        spare = chunk - CAP * tail
        if spare:
            tails = tails + [jnp.zeros((total.shape[0], spare), F32)]
        return total + jnp.concatenate(tails, axis=1)

    def pack(u, mask, pieces, source, scale):
        picked = [ones(mask & piece) for piece in pieces]
        total = jnp.zeros((width, chunk), F32)
        for j, (at, size) in enumerate(spans):
            total = total + mm(picked[j], source[:, at:at + size])
        tails = [mm(picked[FOLD + c], source[:, cut:]) for c in range(CAP)]
        if scale is not None:
            total = total * scale(pieces[0] | pieces[1] | pieces[2])
            tails = [part * scale(pieces[FOLD + c]) for c, part in enumerate(tails)]
        snd[u] = with_tails(total, tails).astype(BF16).reshape(EXPERTS, BLOCK, chunk)

    width = EXPERTS * BLOCK
    inputs[0].wait()
    first_one, second_one, pieces_one = slots(rt1[...], width, 1)
    inputs[1].wait()
    pack(0, first_one | second_one, pieces_one, tok1, None)

    pl.semaphore_wait(barrier, n + ne - 2)
    order = list(range(1, n))
    for k in order:
        send_copy(0, k).start()
    own_copy(0).start()

    for load in inputs[2:]:
        load.wait()
    first_two, second_two, pieces_two = slots(rt2[...], width, 1)
    pack(1, first_two | second_two, pieces_two, tok2, None)
    for k in order:
        send_copy(1, k).start()
    own_copy(1).start()

    gates = jnp.where(first_two, gt2[0:1, :], 0.0) + jnp.where(second_two, gt2[1:2, :], 0.0)
    pack(2, first_two | second_two, pieces_two, cot2,
         lambda mask: jnp.where(mask, gates, 0.0).sum(axis=1, keepdims=True))
    for k in order:
        send_copy(2, k).start()
    own_copy(2).start()

    count3 = rows3.shape[0]
    for j in range(ne):
        snd3[j, 0:count3, :] = rows3[:, j * span:(j + 1) * span]
        snd3[j, count3:2 * count3, :] = cot3[:, j * span:(j + 1) * span]
    for k in range(1, ne):
        rows_copy(k).start()
    own_rows.start()

    for load in loads:
        load.wait()

    def activations(gate_up):
        gate = gate_up[:, 0:h]
        up = gate_up[:, h:2 * h]
        return gate, up, jax.nn.sigmoid(gate)

    def cotangents(d_hidden, gate, up, sigma):
        d_gate = (d_hidden * up * sigma * (1.0 + gate * (1.0 - sigma))).astype(BF16)
        d_up = (d_hidden * gate * sigma).astype(BF16)
        return d_gate, d_up

    gate_up = jnp.zeros((count3, 2 * h), F32)
    d_hidden = jnp.zeros((count3, h), F32)
    for j, (at, size) in enumerate(spans):
        gate_up = gate_up + mm(rows3[:, at:at + size], wgu[j, 0:size, :])
        d_hidden = d_hidden + mm_nt(cot3[:, at:at + size], wd[j, :, 0:size])
    gate_up = gate_up + mm(rows3[:, cut:], wgu_tail[...])
    d_hidden = d_hidden + mm_nt(cot3[:, cut:], wd_tail[...])
    gate, up, sigma = activations(gate_up)
    d_gate, d_up = cotangents(d_hidden, gate, up, sigma)
    fac_snd[:, 0:h] = d_gate
    fac_snd[:, h:2 * h] = d_up
    fac_snd[:, 2 * h:3 * h] = (gate * sigma * up).astype(BF16)
    for k in range(1, ne):
        factor_copy(k).start()
    own_factors.start()

    rows = GROUP * BLOCK
    row = lax.broadcasted_iota(jnp.int32, (rows, rows), 0)
    column = lax.broadcasted_iota(jnp.int32, (rows, rows), 1)
    same = row // BLOCK == column // BLOCK
    to, of = row % BLOCK, column % BLOCK
    slot_row = same & (to < FOLD * CAP)
    from_tail = slot_row & (of == FOLD * CAP)
    join = jnp.concatenate(
        [jnp.where(slot_row & (of < FOLD * CAP) & (to % CAP == of % CAP), 1.0, 0.0)]
        + [jnp.where(from_tail & (to % CAP == c), 1.0, 0.0) for c in range(CAP)], axis=1)
    to_tail = [ones(same & (to == FOLD * CAP) & (of == c)) for c in range(CAP)]

    def chunk_mask(j, size):
        slot = lax.broadcasted_iota(jnp.int32, (rows, size), 0) % BLOCK
        return slot // CAP == j

    def joined(parts, tails):
        total = jnp.zeros_like(parts[0])
        for j, part in enumerate(parts):
            total = total + jnp.where(chunk_mask(j, part.shape[1]), part, 0.0)
        total = jnp.concatenate([total] + tails, axis=0)
        return jnp.dot(join, total, precision=lax.Precision.HIGHEST, preferred_element_type=F32)

    def spread(value, j):
        return jnp.where(chunk_mask(j, value.shape[1]), value, 0.0).astype(BF16)

    def groups(body):
        if n == GROUP:
            body(0)
        else:
            pl.loop(0, n // GROUP)(lambda b: body(b * GROUP))

    def block(ref, u, b):
        return ref[u, pl.ds(b, GROUP)].reshape(rows, chunk)

    def tails_of(x):
        return [x[:, c * tail:(c + 1) * tail] for c in range(CAP)]

    def gate_ups(x):
        return joined(
            [mm(x, wgu[j]) for j in range(FOLD)], [mm(part, wgu_tail[...]) for part in tails_of(x)])

    def answer_with(total, last):
        last = last.astype(BF16)
        whole = with_tails(total, [mm(place, last) for place in to_tail])
        return whole.astype(BF16).reshape(GROUP, BLOCK, chunk)

    def forward(b):
        gate, up, sigma = activations(gate_ups(block(rcv, 0, b)))
        hidden = gate * sigma * up
        total = sum(mm(spread(hidden, j), wd[j]) for j in range(FOLD))
        ret_snd[0, pl.ds(b, GROUP)] = answer_with(total, mm(hidden.astype(BF16), wd_tail[...]))

    def backward(b):
        y = block(rcv, 2, b)
        gate, up, sigma = activations(gate_ups(block(rcv, 1, b)))
        d_hidden = joined(
            [mm_nt(y, wd[j]) for j in range(FOLD)], [mm_nt(part, wd_tail[...]) for part in tails_of(y)])
        both = jnp.concatenate(cotangents(d_hidden, gate, up, sigma), axis=1)
        total = sum(mm_nt(spread(both.astype(F32), j), wgu[j]) for j in range(FOLD))
        ret_snd[1, pl.ds(b, GROUP)] = answer_with(total, mm_nt(both, wgu_tail[...]))

    for k in order:
        send_copy(0, k).wait_recv()
    own_copy(0).wait()
    groups(forward)
    for k in order:
        ret_copy(0, k).start()
    own_ret(0).start()

    for k in range(1, ne):
        rows_copy(k).wait_recv()
        factor_copy(k).wait_recv()
    own_rows.wait()
    own_factors.wait()
    all_rows = rcv3[:, 0:count3, :].reshape(ne * count3, span)
    all_cots = rcv3[:, count3:2 * count3, :].reshape(ne * count3, span)
    factors = fac_rcv[...].reshape(ne * count3, 3 * h)
    pair = mm_tn(all_rows, factors[:, 0:2 * h]).astype(BF16)
    grads_buf[0] = pair[:, 0:h]
    grads_buf[1] = pair[:, h:2 * h]
    grads_buf[2] = mm_tn(all_cots, factors[:, 2 * h:3 * h]).astype(BF16)

    stores = [
        pltpu.make_async_copy(source, target, out_sem.at[i])
        for i, (source, target) in enumerate(((grads_buf, grads), (out1_buf, out1), (dx2_buf, dx2)))]
    stores[0].start()

    for u in (1, 2):
        for k in order:
            send_copy(u, k).wait_recv()
        own_copy(u).wait()
    groups(backward)
    for k in order:
        ret_copy(1, k).start()
    own_ret(1).start()

    back = n * BLOCK
    first, second, masks = slots(rt1[...], back, slices)
    weight = jnp.where(first, gt1[0:1, :], 0.0) + jnp.where(second, gt1[1:2, :], 0.0)
    pieces = []
    for mask in masks:
        rest = jnp.where(mask, weight, 0.0)
        split = []
        for _ in range(3):
            split.append(rest.astype(BF16))
            rest = rest - split[-1].astype(F32)
        pieces.append(jnp.concatenate([turned(piece) for piece in split], axis=0))
    first, second, masks = slots(rt2[...], back, slices)
    picked = [turned(ones((first | second) & mask)) for mask in masks]

    def unpacked(weights, answer):
        yield from ((at, size, mm(weights[j], answer)) for j, (at, size) in enumerate(spans))
        yield cut, tail, sum(mm(weights[FOLD + c], part) for c, part in enumerate(tails_of(answer)))

    for k in order:
        ret_copy(0, k).wait_recv()
    own_ret(0).wait()
    for at, size, result in unpacked(pieces, ret_rcv[0].reshape(back, chunk)):
        out1_buf[:, at:at + size] = (
            result[0:BLOCK] + result[BLOCK:2 * BLOCK] + result[2 * BLOCK:3 * BLOCK]).astype(BF16)
    stores[1].start()

    for k in order:
        ret_copy(1, k).wait_recv()
    own_ret(1).wait()
    for at, size, result in unpacked(picked, ret_rcv[1].reshape(back, chunk)):
        dx2_buf[:, at:at + size] = result.astype(BF16)
    stores[2].start()

    for k in order:
        for u in range(3):
            send_copy(u, k).wait_send()
        for u in range(2):
            ret_copy(u, k).wait_send()
    for k in range(1, ne):
        rows_copy(k).wait_send()
        factor_copy(k).wait_send()
    for copy in stores:
        copy.wait()


def store(a, b, c, a_out, b_out, c_out, sem):
    copies = [
        pltpu.make_async_copy(source, target, sem.at[i])
        for i, (source, target) in enumerate(((a, a_out), (b, b_out), (c, c_out)))]
    for copy in copies:
        copy.start()
    for copy in copies:
        copy.wait()


def shards(*args):
    args = [arg.T if i in (1, 2, 4, 5) else arg for i, arg in enumerate(args)]
    n = lax.axis_size("expert")
    ne = lax.axis_size("edata")
    tokens, depth = args[0].shape
    count3 = args[7].shape[0]
    h = args[9].shape[1]
    span = depth // ne
    chunk = depth // (FOLD * 128) * 128
    tail = depth - FOLD * chunk
    hbm = pl.BlockSpec(memory_space=pl.ANY)
    results = (
            jax.ShapeDtypeStruct((tokens, depth), BF16),
            jax.ShapeDtypeStruct((tokens, depth), BF16),
            jax.ShapeDtypeStruct((3, span, h), BF16),
    )
    landed = pl.pallas_call(
        functools.partial(kernel, n, ne),
        out_shape=results,
        in_specs=[hbm] * 12,
        out_specs=(hbm,) * 3,
        scratch_shapes=[pltpu.VMEM(arg.shape, arg.dtype) for arg in args[:9]] + [
            pltpu.SemaphoreType.DMA((9,)),
            pltpu.VMEM((tokens, depth), BF16),
            pltpu.VMEM((tokens, depth), BF16),
            pltpu.VMEM((3, span, h), BF16),
            pltpu.SemaphoreType.DMA((3,)),
            pltpu.VMEM((tail, 2 * h), BF16),
            pltpu.VMEM((h, tail), BF16),
            pltpu.VMEM((FOLD, chunk, 2 * h), BF16),
            pltpu.VMEM((FOLD, h, chunk), BF16),
            pltpu.VMEM((3, EXPERTS, BLOCK, chunk), BF16),
            pltpu.VMEM((3, n, BLOCK, chunk), BF16),
            pltpu.VMEM((2, n, BLOCK, chunk), BF16),
            pltpu.VMEM((2, n, BLOCK, chunk), BF16),
            pltpu.VMEM((ne, 2 * count3, span), BF16),
            pltpu.VMEM((ne, 2 * count3, span), BF16),
            pltpu.VMEM((count3, 3 * h), BF16),
            pltpu.VMEM((ne, count3, 3 * h), BF16),
            pltpu.SemaphoreType.DMA((3 * FOLD + 3,)),
            pltpu.SemaphoreType.DMA((7,)),
            pltpu.SemaphoreType.DMA((3, n)),
            pltpu.SemaphoreType.DMA((3, n)),
            pltpu.SemaphoreType.DMA((2, n)),
            pltpu.SemaphoreType.DMA((2, n)),
            pltpu.SemaphoreType.DMA((2, ne)),
            pltpu.SemaphoreType.DMA((2, ne)),
        ],
        compiler_params=pltpu.CompilerParams(
            collective_id=0, has_side_effects=True, vmem_limit_bytes=62 * 2**20),
    )(*args)
    out_one, dx_two, grads = pl.pallas_call(
        store,
        out_shape=results,
        in_specs=[hbm] * 3,
        out_specs=(hbm,) * 3,
        scratch_shapes=[pltpu.SemaphoreType.DMA((3,))],
        compiler_params=pltpu.CompilerParams(vmem_limit_bytes=62 * 2**20),
    )(*landed)
    return out_one, dx_two, jnp.transpose(grads, (1, 0, 2))


def solution(mesh):
    both = P(("edata", "expert"), None)
    return jax.shard_map(
        shards,
        mesh=mesh,
        in_specs=(both,) * 9 + (P(None, "expert"), P(None, "expert"), P("expert", None)),
        out_specs=(both, both, P("edata", None, "expert")),
        check_vma=False,
    )
```

```python
import functools

import jax
import jax.numpy as jnp
from jax import lax
from jax.experimental import pallas as pl
from jax.experimental.pallas import tpu as pltpu
from jax.sharding import PartitionSpec as P

EXPERTS = 8
CAP = 5
BLOCK = 16
FOLD = 3
GROUP = 8
BF16 = jnp.bfloat16
F32 = jnp.float32
MESH = pl.DeviceIdType.MESH


def mm(a, b):
    return jnp.dot(a, b, preferred_element_type=F32)


def mm_nt(a, b):
    return lax.dot_general(a, b, (((1,), (1,)), ((), ())), preferred_element_type=F32)


def mm_tn(a, b):
    return lax.dot_general(a, b, (((0,), (0,)), ((), ())), preferred_element_type=F32)


def slots(routes, width, slices):
    count = routes.shape[1]
    row = lax.broadcasted_iota(jnp.int32, (width, count), 0)
    expert = row // (BLOCK * slices)
    at = row % BLOCK
    first = routes[0:1, :] == expert
    second = routes[1:2, :] == expert
    named = jnp.where(first | second, 1.0, 0.0).astype(BF16)
    earlier = lax.broadcasted_iota(jnp.int32, (count, count), 0)
    later = lax.broadcasted_iota(jnp.int32, (count, count), 1)
    before = jnp.where(earlier < later, 1.0, 0.0).astype(BF16)
    position = mm(named, before)
    here = position == (at % CAP).astype(F32)
    pieces = [here & (at // CAP == j) for j in range(FOLD)]
    pieces += [(position == float(c)) & (at == FOLD * CAP) for c in range(CAP)]
    return first, second, pieces


def turned(piece):
    count = piece.shape[1]
    row = lax.broadcasted_iota(jnp.int32, (count, count), 0)
    column = lax.broadcasted_iota(jnp.int32, (count, count), 1)
    return mm_nt(jnp.where(row == column, 1.0, 0.0).astype(BF16), piece).astype(BF16)


def ones(mask):
    return jnp.where(mask, 1.0, 0.0).astype(BF16)


def kernel(
    n, ne, tok1_hbm, rt1_hbm, gt1_hbm, tok2_hbm, rt2_hbm, gt2_hbm, cot2_hbm, rows3_hbm, cot3_hbm,
    wg_hbm, wu_hbm, wd_hbm,
    out1, dx2, grads,
    tok1, rt1, gt1, tok2, rt2, gt2, cot2, rows3, cot3, in_sem,
    out1_buf, dx2_buf, grads_buf, out_sem, wgu_tail, wd_tail,
    wgu, wd, snd, rcv, ret_snd, ret_rcv, snd3, rcv3, fac_snd, fac_rcv,
    w_sem, own_sem, snd_sem, rcv_sem, ret_snd_sem, ret_rcv_sem, e_snd_sem, e_rcv_sem,
):
    depth = tok1.shape[1]
    h = wd.shape[1]
    chunk = wd.shape[2]
    slices = n // EXPERTS
    span = depth // ne
    spans = [(j * chunk, chunk) for j in range(FOLD)]
    cut = FOLD * chunk
    tail = depth - cut
    me = lax.axis_index("expert")
    mine = lax.axis_index("edata")

    def expert_peer(k):
        return lax.rem(me + k, n)

    def edata_peer(k):
        return lax.rem(mine + k, ne)

    barrier = pltpu.get_barrier_semaphore()
    for k in range(1, n):
        pl.semaphore_signal(barrier, inc=1, device_id=(mine, expert_peer(k)), device_id_type=MESH)
    for k in range(1, ne):
        pl.semaphore_signal(barrier, inc=1, device_id=(edata_peer(k), me), device_id_type=MESH)

    pairs = (
        (rt1_hbm, rt1), (tok1_hbm, tok1), (rt2_hbm, rt2), (tok2_hbm, tok2), (gt2_hbm, gt2),
        (cot2_hbm, cot2), (gt1_hbm, gt1), (rows3_hbm, rows3), (cot3_hbm, cot3))
    inputs = [pltpu.make_async_copy(a, b, in_sem.at[i]) for i, (a, b) in enumerate(pairs)]
    for load in inputs:
        load.start()
    loads = []
    for j, (at, size) in enumerate(spans):
        loads.append(pltpu.make_async_copy(
            wg_hbm.at[pl.ds(at, size), :], wgu.at[j, pl.ds(0, size), pl.ds(0, h)], w_sem.at[len(loads)]))
        loads.append(pltpu.make_async_copy(
            wu_hbm.at[pl.ds(at, size), :], wgu.at[j, pl.ds(0, size), pl.ds(h, h)], w_sem.at[len(loads)]))
        loads.append(pltpu.make_async_copy(
            wd_hbm.at[:, pl.ds(at, size)], wd.at[j, :, pl.ds(0, size)], w_sem.at[len(loads)]))
    for source, target in (
        (wg_hbm.at[pl.ds(cut, tail), :], wgu_tail.at[:, pl.ds(0, h)]),
        (wu_hbm.at[pl.ds(cut, tail), :], wgu_tail.at[:, pl.ds(h, h)]),
        (wd_hbm.at[:, pl.ds(cut, tail)], wd_tail),
    ):
        loads.append(pltpu.make_async_copy(source, target, w_sem.at[len(loads)]))
    for load in loads:
        load.start()
    def send_copy(u, k):
        peer = expert_peer(k)
        return pltpu.make_async_remote_copy(
            src_ref=snd.at[u, peer // slices], dst_ref=rcv.at[u, me],
            send_sem=snd_sem.at[u, k], recv_sem=rcv_sem.at[u, k],
            device_id=(mine, peer), device_id_type=MESH)

    def own_copy(u):
        return pltpu.make_async_copy(snd.at[u, me // slices], rcv.at[u, me], own_sem.at[u])

    def ret_copy(u, k):
        peer = expert_peer(k)
        return pltpu.make_async_remote_copy(
            src_ref=ret_snd.at[u, peer], dst_ref=ret_rcv.at[u, me],
            send_sem=ret_snd_sem.at[u, k], recv_sem=ret_rcv_sem.at[u, k],
            device_id=(mine, peer), device_id_type=MESH)

    def own_ret(u):
        return pltpu.make_async_copy(ret_snd.at[u, me], ret_rcv.at[u, me], own_sem.at[3 + u])

    def rows_copy(k):
        peer = edata_peer(k)
        return pltpu.make_async_remote_copy(
            src_ref=snd3.at[peer], dst_ref=rcv3.at[mine],
            send_sem=e_snd_sem.at[0, k], recv_sem=e_rcv_sem.at[0, k],
            device_id=(peer, me), device_id_type=MESH)

    def factor_copy(k):
        return pltpu.make_async_remote_copy(
            src_ref=fac_snd, dst_ref=fac_rcv.at[mine],
            send_sem=e_snd_sem.at[1, k], recv_sem=e_rcv_sem.at[1, k],
            device_id=(edata_peer(k), me), device_id_type=MESH)

    own_rows = pltpu.make_async_copy(snd3.at[mine], rcv3.at[mine], own_sem.at[5])
    own_factors = pltpu.make_async_copy(fac_snd, fac_rcv.at[mine], own_sem.at[6])

    def with_tails(total, tails):
        spare = chunk - CAP * tail
        if spare:
            tails = tails + [jnp.zeros((total.shape[0], spare), F32)]
        return total + jnp.concatenate(tails, axis=1)

    def pack(u, mask, pieces, source, scale):
        picked = [ones(mask & piece) for piece in pieces]
        total = jnp.zeros((width, chunk), F32)
        for j, (at, size) in enumerate(spans):
            total = total + mm(picked[j], source[:, at:at + size])
        tails = [mm(picked[FOLD + c], source[:, cut:]) for c in range(CAP)]
        if scale is not None:
            total = total * scale(pieces[0] | pieces[1] | pieces[2])
            tails = [part * scale(pieces[FOLD + c]) for c, part in enumerate(tails)]
        snd[u] = with_tails(total, tails).astype(BF16).reshape(EXPERTS, BLOCK, chunk)

    width = EXPERTS * BLOCK
    inputs[0].wait()
    first_one, second_one, pieces_one = slots(rt1[...], width, 1)
    inputs[1].wait()
    pack(0, first_one | second_one, pieces_one, tok1, None)

    pl.semaphore_wait(barrier, n + ne - 2)
    order = sorted(range(1, n), key=lambda k: abs(2 * k - n))
    for k in order:
        send_copy(0, k).start()
    own_copy(0).start()

    for load in inputs[2:]:
        load.wait()
    first_two, second_two, pieces_two = slots(rt2[...], width, 1)
    pack(1, first_two | second_two, pieces_two, tok2, None)
    for k in order:
        send_copy(1, k).start()
    own_copy(1).start()

    gates = jnp.where(first_two, gt2[0:1, :], 0.0) + jnp.where(second_two, gt2[1:2, :], 0.0)
    pack(2, first_two | second_two, pieces_two, cot2,
         lambda mask: jnp.where(mask, gates, 0.0).sum(axis=1, keepdims=True))
    for k in order:
        send_copy(2, k).start()
    own_copy(2).start()

    count3 = rows3.shape[0]
    for j in range(ne):
        snd3[j, 0:count3, :] = rows3[:, j * span:(j + 1) * span]
        snd3[j, count3:2 * count3, :] = cot3[:, j * span:(j + 1) * span]
    for k in range(1, ne):
        rows_copy(k).start()
    own_rows.start()

    for load in loads:
        load.wait()

    def activations(gate_up):
        gate = gate_up[:, 0:h]
        up = gate_up[:, h:2 * h]
        return gate, up, jax.nn.sigmoid(gate)

    def cotangents(d_hidden, gate, up, sigma):
        d_gate = (d_hidden * up * sigma * (1.0 + gate * (1.0 - sigma))).astype(BF16)
        d_up = (d_hidden * gate * sigma).astype(BF16)
        return d_gate, d_up

    gate_up = jnp.zeros((count3, 2 * h), F32)
    d_hidden = jnp.zeros((count3, h), F32)
    for j, (at, size) in enumerate(spans):
        gate_up = gate_up + mm(rows3[:, at:at + size], wgu[j, 0:size, :])
        d_hidden = d_hidden + mm_nt(cot3[:, at:at + size], wd[j, :, 0:size])
    gate_up = gate_up + mm(rows3[:, cut:], wgu_tail[...])
    d_hidden = d_hidden + mm_nt(cot3[:, cut:], wd_tail[...])
    gate, up, sigma = activations(gate_up)
    d_gate, d_up = cotangents(d_hidden, gate, up, sigma)
    fac_snd[:, 0:h] = d_gate
    fac_snd[:, h:2 * h] = d_up
    fac_snd[:, 2 * h:3 * h] = (gate * sigma * up).astype(BF16)
    for k in range(1, ne):
        factor_copy(k).start()
    own_factors.start()

    rows = GROUP * BLOCK
    row = lax.broadcasted_iota(jnp.int32, (rows, rows), 0)
    column = lax.broadcasted_iota(jnp.int32, (rows, rows), 1)
    same = row // BLOCK == column // BLOCK
    to, of = row % BLOCK, column % BLOCK
    slot_row = same & (to < FOLD * CAP)
    from_tail = slot_row & (of == FOLD * CAP)
    join = jnp.concatenate(
        [jnp.where(slot_row & (of < FOLD * CAP) & (to % CAP == of % CAP), 1.0, 0.0)]
        + [jnp.where(from_tail & (to % CAP == c), 1.0, 0.0) for c in range(CAP)], axis=1)
    to_tail = [ones(same & (to == FOLD * CAP) & (of == c)) for c in range(CAP)]

    def chunk_mask(j, size):
        slot = lax.broadcasted_iota(jnp.int32, (rows, size), 0) % BLOCK
        return slot // CAP == j

    def joined(parts, tails):
        total = jnp.zeros_like(parts[0])
        for j, part in enumerate(parts):
            total = total + jnp.where(chunk_mask(j, part.shape[1]), part, 0.0)
        total = jnp.concatenate([total] + tails, axis=0)
        return jnp.dot(join, total, precision=lax.Precision.HIGHEST, preferred_element_type=F32)

    def spread(value, j):
        return jnp.where(chunk_mask(j, value.shape[1]), value, 0.0).astype(BF16)

    def groups(body):
        if n == GROUP:
            body(0)
        else:
            pl.loop(0, n // GROUP)(lambda b: body(b * GROUP))

    def block(ref, u, b):
        return ref[u, pl.ds(b, GROUP)].reshape(rows, chunk)

    def tails_of(x):
        return [x[:, c * tail:(c + 1) * tail] for c in range(CAP)]

    def gate_ups(x):
        return joined(
            [mm(x, wgu[j]) for j in range(FOLD)], [mm(part, wgu_tail[...]) for part in tails_of(x)])

    def answer_with(total, last):
        last = last.astype(BF16)
        whole = with_tails(total, [mm(place, last) for place in to_tail])
        return whole.astype(BF16).reshape(GROUP, BLOCK, chunk)

    def forward(b):
        gate, up, sigma = activations(gate_ups(block(rcv, 0, b)))
        hidden = gate * sigma * up
        total = sum(mm(spread(hidden, j), wd[j]) for j in range(FOLD))
        ret_snd[0, pl.ds(b, GROUP)] = answer_with(total, mm(hidden.astype(BF16), wd_tail[...]))

    def backward(b):
        y = block(rcv, 2, b)
        gate, up, sigma = activations(gate_ups(block(rcv, 1, b)))
        d_hidden = joined(
            [mm_nt(y, wd[j]) for j in range(FOLD)], [mm_nt(part, wd_tail[...]) for part in tails_of(y)])
        both = jnp.concatenate(cotangents(d_hidden, gate, up, sigma), axis=1)
        total = sum(mm_nt(spread(both.astype(F32), j), wgu[j]) for j in range(FOLD))
        ret_snd[1, pl.ds(b, GROUP)] = answer_with(total, mm_nt(both, wgu_tail[...]))

    for k in order:
        send_copy(0, k).wait_recv()
    own_copy(0).wait()
    groups(forward)
    for k in order:
        ret_copy(0, k).start()
    own_ret(0).start()

    for k in range(1, ne):
        rows_copy(k).wait_recv()
        factor_copy(k).wait_recv()
    own_rows.wait()
    own_factors.wait()
    all_rows = rcv3[:, 0:count3, :].reshape(ne * count3, span)
    all_cots = rcv3[:, count3:2 * count3, :].reshape(ne * count3, span)
    factors = fac_rcv[...].reshape(ne * count3, 3 * h)
    pair = mm_tn(all_rows, factors[:, 0:2 * h]).astype(BF16)
    grads_buf[0] = pair[:, 0:h]
    grads_buf[1] = pair[:, h:2 * h]
    grads_buf[2] = mm_tn(all_cots, factors[:, 2 * h:3 * h]).astype(BF16)

    stores = [
        pltpu.make_async_copy(source, target, out_sem.at[i])
        for i, (source, target) in enumerate(((grads_buf, grads), (out1_buf, out1), (dx2_buf, dx2)))]
    stores[0].start()

    for u in (1, 2):
        for k in order:
            send_copy(u, k).wait_recv()
        own_copy(u).wait()
    groups(backward)
    for k in order:
        ret_copy(1, k).start()
    own_ret(1).start()

    back = n * BLOCK
    first, second, masks = slots(rt1[...], back, slices)
    weight = jnp.where(first, gt1[0:1, :], 0.0) + jnp.where(second, gt1[1:2, :], 0.0)
    pieces = []
    for mask in masks:
        rest = jnp.where(mask, weight, 0.0)
        split = []
        for _ in range(3):
            split.append(rest.astype(BF16))
            rest = rest - split[-1].astype(F32)
        pieces.append(jnp.concatenate([turned(piece) for piece in split], axis=0))
    first, second, masks = slots(rt2[...], back, slices)
    picked = [turned(ones((first | second) & mask)) for mask in masks]

    def unpacked(weights, answer):
        yield from ((at, size, mm(weights[j], answer)) for j, (at, size) in enumerate(spans))
        yield cut, tail, sum(mm(weights[FOLD + c], part) for c, part in enumerate(tails_of(answer)))

    for k in order:
        ret_copy(0, k).wait_recv()
    own_ret(0).wait()
    for at, size, result in unpacked(pieces, ret_rcv[0].reshape(back, chunk)):
        out1_buf[:, at:at + size] = (
            result[0:BLOCK] + result[BLOCK:2 * BLOCK] + result[2 * BLOCK:3 * BLOCK]).astype(BF16)
    stores[1].start()

    for k in order:
        ret_copy(1, k).wait_recv()
    own_ret(1).wait()
    for at, size, result in unpacked(picked, ret_rcv[1].reshape(back, chunk)):
        dx2_buf[:, at:at + size] = result.astype(BF16)
    stores[2].start()

    for k in order:
        for u in range(3):
            send_copy(u, k).wait_send()
        for u in range(2):
            ret_copy(u, k).wait_send()
    for k in range(1, ne):
        rows_copy(k).wait_send()
        factor_copy(k).wait_send()
    for copy in stores:
        copy.wait()


def store(a, b, c, a_out, b_out, c_out, a_buf, b_buf, c_buf, in_sem, out_sem):
    triples = [(c.at[i], c_buf.at[i], c_out.at[i]) for i in range(c.shape[0])]
    triples += [(a, a_buf, a_out), (b, b_buf, b_out)]
    loads = [pltpu.make_async_copy(t[0], t[1], in_sem.at[i]) for i, t in enumerate(triples)]
    saves = [pltpu.make_async_copy(t[1], t[2], out_sem.at[i]) for i, t in enumerate(triples)]
    for load in loads:
        load.start()
    for load, save in zip(loads, saves):
        load.wait()
        save.start()
    for save in saves:
        save.wait()


def shards(*args):
    args = [arg.T if i in (1, 2, 4, 5) else arg for i, arg in enumerate(args)]
    n = lax.axis_size("expert")
    ne = lax.axis_size("edata")
    tokens, depth = args[0].shape
    count3 = args[7].shape[0]
    h = args[9].shape[1]
    span = depth // ne
    chunk = depth // (FOLD * 128) * 128
    tail = depth - FOLD * chunk
    hbm = pl.BlockSpec(memory_space=pl.ANY)
    results = (
            jax.ShapeDtypeStruct((tokens, depth), BF16),
            jax.ShapeDtypeStruct((tokens, depth), BF16),
            jax.ShapeDtypeStruct((3, span, h), BF16),
    )
    landed = pl.pallas_call(
        functools.partial(kernel, n, ne),
        out_shape=results,
        in_specs=[hbm] * 12,
        out_specs=(hbm,) * 3,
        scratch_shapes=[pltpu.VMEM(arg.shape, arg.dtype) for arg in args[:9]] + [
            pltpu.SemaphoreType.DMA((9,)),
            pltpu.VMEM((tokens, depth), BF16),
            pltpu.VMEM((tokens, depth), BF16),
            pltpu.VMEM((3, span, h), BF16),
            pltpu.SemaphoreType.DMA((3,)),
            pltpu.VMEM((tail, 2 * h), BF16),
            pltpu.VMEM((h, tail), BF16),
            pltpu.VMEM((FOLD, chunk, 2 * h), BF16),
            pltpu.VMEM((FOLD, h, chunk), BF16),
            pltpu.VMEM((3, EXPERTS, BLOCK, chunk), BF16),
            pltpu.VMEM((3, n, BLOCK, chunk), BF16),
            pltpu.VMEM((2, n, BLOCK, chunk), BF16),
            pltpu.VMEM((2, n, BLOCK, chunk), BF16),
            pltpu.VMEM((ne, 2 * count3, span), BF16),
            pltpu.VMEM((ne, 2 * count3, span), BF16),
            pltpu.VMEM((count3, 3 * h), BF16),
            pltpu.VMEM((ne, count3, 3 * h), BF16),
            pltpu.SemaphoreType.DMA((3 * FOLD + 3,)),
            pltpu.SemaphoreType.DMA((7,)),
            pltpu.SemaphoreType.DMA((3, n)),
            pltpu.SemaphoreType.DMA((3, n)),
            pltpu.SemaphoreType.DMA((2, n)),
            pltpu.SemaphoreType.DMA((2, n)),
            pltpu.SemaphoreType.DMA((2, ne)),
            pltpu.SemaphoreType.DMA((2, ne)),
        ],
        compiler_params=pltpu.CompilerParams(
            collective_id=0, has_side_effects=True, vmem_limit_bytes=62 * 2**20),
    )(*args)
    out_one, dx_two, grads = pl.pallas_call(
        store,
        out_shape=results,
        in_specs=[hbm] * 3,
        out_specs=(hbm,) * 3,
        scratch_shapes=[pltpu.VMEM(result.shape, result.dtype) for result in results]
        + [pltpu.SemaphoreType.DMA((5,)), pltpu.SemaphoreType.DMA((5,))],
        compiler_params=pltpu.CompilerParams(vmem_limit_bytes=62 * 2**20),
    )(*landed)
    return out_one, dx_two, jnp.transpose(grads, (1, 0, 2))


def solution(mesh):
    both = P(("edata", "expert"), None)
    return jax.shard_map(
        shards,
        mesh=mesh,
        in_specs=(both,) * 9 + (P(None, "expert"), P(None, "expert"), P("expert", None)),
        out_specs=(both, both, P("edata", None, "expert")),
        check_vma=False,
    )
```

```python
import functools

import jax
import jax.numpy as jnp
from jax import lax
from jax.experimental import pallas as pl
from jax.experimental.pallas import tpu as pltpu
from jax.sharding import PartitionSpec as P

EXPERTS = 8
CAP = 5
BLOCK = 16
FOLD = 3
GROUP = 8
BF16 = jnp.bfloat16
F32 = jnp.float32
MESH = pl.DeviceIdType.MESH


def mm(a, b):
    return jnp.dot(a, b, preferred_element_type=F32)


def mm_nt(a, b):
    return lax.dot_general(a, b, (((1,), (1,)), ((), ())), preferred_element_type=F32)


def mm_tn(a, b):
    return lax.dot_general(a, b, (((0,), (0,)), ((), ())), preferred_element_type=F32)


def slots(routes, width, slices):
    count = routes.shape[1]
    row = lax.broadcasted_iota(jnp.int32, (width, count), 0)
    expert = row // (BLOCK * slices)
    at = row % BLOCK
    first = routes[0:1, :] == expert
    second = routes[1:2, :] == expert
    named = jnp.where(first | second, 1.0, 0.0).astype(BF16)
    earlier = lax.broadcasted_iota(jnp.int32, (count, count), 0)
    later = lax.broadcasted_iota(jnp.int32, (count, count), 1)
    before = jnp.where(earlier < later, 1.0, 0.0).astype(BF16)
    position = mm(named, before)
    here = position == (at % CAP).astype(F32)
    pieces = [here & (at // CAP == j) for j in range(FOLD)]
    pieces += [(position == float(c)) & (at == FOLD * CAP) for c in range(CAP)]
    return first, second, pieces


def turned(piece):
    count = piece.shape[1]
    row = lax.broadcasted_iota(jnp.int32, (count, count), 0)
    column = lax.broadcasted_iota(jnp.int32, (count, count), 1)
    return mm_nt(jnp.where(row == column, 1.0, 0.0).astype(BF16), piece).astype(BF16)


def ones(mask):
    return jnp.where(mask, 1.0, 0.0).astype(BF16)


def kernel(
    n, ne, tok1_hbm, rt1_hbm, gt1_hbm, tok2_hbm, rt2_hbm, gt2_hbm, cot2_hbm, rows3_hbm, cot3_hbm,
    wg_hbm, wu_hbm, wd_hbm,
    out1, dx2, grads,
    tok1, rt1, gt1, tok2, rt2, gt2, cot2, rows3, cot3, in_sem,
    out1_buf, dx2_buf, grads_buf, out_sem, wgu_tail, wd_tail,
    wgu, wd, snd, rcv, ret_snd, ret_rcv, snd3, rcv3, fac_snd, fac_rcv,
    w_sem, own_sem, snd_sem, rcv_sem, ret_snd_sem, ret_rcv_sem, e_snd_sem, e_rcv_sem,
):
    depth = tok1.shape[1]
    h = wd.shape[1]
    chunk = wd.shape[2]
    slices = n // EXPERTS
    span = depth // ne
    spans = [(j * chunk, chunk) for j in range(FOLD)]
    cut = FOLD * chunk
    tail = depth - cut
    me = lax.axis_index("expert")
    mine = lax.axis_index("edata")

    def expert_peer(k):
        return lax.rem(me + k, n)

    def edata_peer(k):
        return lax.rem(mine + k, ne)

    barrier = pltpu.get_barrier_semaphore()
    for k in range(1, n):
        pl.semaphore_signal(barrier, inc=1, device_id=(mine, expert_peer(k)), device_id_type=MESH)
    for k in range(1, ne):
        pl.semaphore_signal(barrier, inc=1, device_id=(edata_peer(k), me), device_id_type=MESH)

    pairs = (
        (rt1_hbm, rt1), (tok1_hbm, tok1), (rt2_hbm, rt2), (tok2_hbm, tok2), (gt2_hbm, gt2),
        (cot2_hbm, cot2), (gt1_hbm, gt1), (rows3_hbm, rows3), (cot3_hbm, cot3))
    inputs = [pltpu.make_async_copy(a, b, in_sem.at[i]) for i, (a, b) in enumerate(pairs)]
    for load in inputs:
        load.start()
    loads = []
    for j, (at, size) in enumerate(spans):
        loads.append(pltpu.make_async_copy(
            wg_hbm.at[pl.ds(at, size), :], wgu.at[j, pl.ds(0, size), pl.ds(0, h)], w_sem.at[len(loads)]))
        loads.append(pltpu.make_async_copy(
            wu_hbm.at[pl.ds(at, size), :], wgu.at[j, pl.ds(0, size), pl.ds(h, h)], w_sem.at[len(loads)]))
        loads.append(pltpu.make_async_copy(
            wd_hbm.at[:, pl.ds(at, size)], wd.at[j, :, pl.ds(0, size)], w_sem.at[len(loads)]))
    for source, target in (
        (wg_hbm.at[pl.ds(cut, tail), :], wgu_tail.at[:, pl.ds(0, h)]),
        (wu_hbm.at[pl.ds(cut, tail), :], wgu_tail.at[:, pl.ds(h, h)]),
        (wd_hbm.at[:, pl.ds(cut, tail)], wd_tail),
    ):
        loads.append(pltpu.make_async_copy(source, target, w_sem.at[len(loads)]))
    for load in loads:
        load.start()
    def send_copy(u, k):
        peer = expert_peer(k)
        return pltpu.make_async_remote_copy(
            src_ref=snd.at[u, peer // slices], dst_ref=rcv.at[u, me],
            send_sem=snd_sem.at[u, k], recv_sem=rcv_sem.at[u, k],
            device_id=(mine, peer), device_id_type=MESH)

    def own_copy(u):
        return pltpu.make_async_copy(snd.at[u, me // slices], rcv.at[u, me], own_sem.at[u])

    def ret_copy(u, k):
        peer = expert_peer(k)
        return pltpu.make_async_remote_copy(
            src_ref=ret_snd.at[u, peer], dst_ref=ret_rcv.at[u, me],
            send_sem=ret_snd_sem.at[u, k], recv_sem=ret_rcv_sem.at[u, k],
            device_id=(mine, peer), device_id_type=MESH)

    def own_ret(u):
        return pltpu.make_async_copy(ret_snd.at[u, me], ret_rcv.at[u, me], own_sem.at[3 + u])

    def rows_copy(k):
        peer = edata_peer(k)
        return pltpu.make_async_remote_copy(
            src_ref=snd3.at[peer], dst_ref=rcv3.at[mine],
            send_sem=e_snd_sem.at[0, k], recv_sem=e_rcv_sem.at[0, k],
            device_id=(peer, me), device_id_type=MESH)

    def factor_copy(k):
        return pltpu.make_async_remote_copy(
            src_ref=fac_snd, dst_ref=fac_rcv.at[mine],
            send_sem=e_snd_sem.at[1, k], recv_sem=e_rcv_sem.at[1, k],
            device_id=(edata_peer(k), me), device_id_type=MESH)

    own_rows = pltpu.make_async_copy(snd3.at[mine], rcv3.at[mine], own_sem.at[5])
    own_factors = pltpu.make_async_copy(fac_snd, fac_rcv.at[mine], own_sem.at[6])

    def with_tails(total, tails):
        spare = chunk - CAP * tail
        if spare:
            tails = tails + [jnp.zeros((total.shape[0], spare), F32)]
        return total + jnp.concatenate(tails, axis=1)

    def pack(u, mask, pieces, source, scale):
        picked = [ones(mask & piece) for piece in pieces]
        total = jnp.zeros((width, chunk), F32)
        for j, (at, size) in enumerate(spans):
            total = total + mm(picked[j], source[:, at:at + size])
        tails = [mm(picked[FOLD + c], source[:, cut:]) for c in range(CAP)]
        if scale is not None:
            total = total * scale(pieces[0] | pieces[1] | pieces[2])
            tails = [part * scale(pieces[FOLD + c]) for c, part in enumerate(tails)]
        snd[u] = with_tails(total, tails).astype(BF16).reshape(EXPERTS, BLOCK, chunk)

    width = EXPERTS * BLOCK
    for load in inputs:
        load.wait()
    first_two, second_two, pieces_two = slots(rt2[...], width, 1)
    pack(1, first_two | second_two, pieces_two, tok2, None)
    pl.semaphore_wait(barrier, n + ne - 2)
    order = sorted(range(1, n), key=lambda k: abs(2 * k - n))
    for k in order:
        send_copy(1, k).start()
    own_copy(1).start()

    gates = jnp.where(first_two, gt2[0:1, :], 0.0) + jnp.where(second_two, gt2[1:2, :], 0.0)
    pack(2, first_two | second_two, pieces_two, cot2,
         lambda mask: jnp.where(mask, gates, 0.0).sum(axis=1, keepdims=True))
    for k in order:
        send_copy(2, k).start()
    own_copy(2).start()

    first_one, second_one, pieces_one = slots(rt1[...], width, 1)
    pack(0, first_one | second_one, pieces_one, tok1, None)

    for k in order:
        send_copy(0, k).start()
    own_copy(0).start()

    count3 = rows3.shape[0]
    for j in range(ne):
        snd3[j, 0:count3, :] = rows3[:, j * span:(j + 1) * span]
        snd3[j, count3:2 * count3, :] = cot3[:, j * span:(j + 1) * span]
    for k in range(1, ne):
        rows_copy(k).start()
    own_rows.start()

    for load in loads:
        load.wait()

    def activations(gate_up):
        gate = gate_up[:, 0:h]
        up = gate_up[:, h:2 * h]
        return gate, up, jax.nn.sigmoid(gate)

    def cotangents(d_hidden, gate, up, sigma):
        d_gate = (d_hidden * up * sigma * (1.0 + gate * (1.0 - sigma))).astype(BF16)
        d_up = (d_hidden * gate * sigma).astype(BF16)
        return d_gate, d_up

    gate_up = jnp.zeros((count3, 2 * h), F32)
    d_hidden = jnp.zeros((count3, h), F32)
    for j, (at, size) in enumerate(spans):
        gate_up = gate_up + mm(rows3[:, at:at + size], wgu[j, 0:size, :])
        d_hidden = d_hidden + mm_nt(cot3[:, at:at + size], wd[j, :, 0:size])
    gate_up = gate_up + mm(rows3[:, cut:], wgu_tail[...])
    d_hidden = d_hidden + mm_nt(cot3[:, cut:], wd_tail[...])
    gate, up, sigma = activations(gate_up)
    d_gate, d_up = cotangents(d_hidden, gate, up, sigma)
    fac_snd[:, 0:h] = d_gate
    fac_snd[:, h:2 * h] = d_up
    fac_snd[:, 2 * h:3 * h] = (gate * sigma * up).astype(BF16)
    for k in range(1, ne):
        factor_copy(k).start()
    own_factors.start()

    rows = GROUP * BLOCK
    row = lax.broadcasted_iota(jnp.int32, (rows, rows), 0)
    column = lax.broadcasted_iota(jnp.int32, (rows, rows), 1)
    same = row // BLOCK == column // BLOCK
    to, of = row % BLOCK, column % BLOCK
    slot_row = same & (to < FOLD * CAP)
    from_tail = slot_row & (of == FOLD * CAP)
    join = jnp.concatenate(
        [jnp.where(slot_row & (of < FOLD * CAP) & (to % CAP == of % CAP), 1.0, 0.0)]
        + [jnp.where(from_tail & (to % CAP == c), 1.0, 0.0) for c in range(CAP)], axis=1)
    to_tail = [ones(same & (to == FOLD * CAP) & (of == c)) for c in range(CAP)]

    def chunk_mask(j, size):
        slot = lax.broadcasted_iota(jnp.int32, (rows, size), 0) % BLOCK
        return slot // CAP == j

    def joined(parts, tails):
        total = jnp.zeros_like(parts[0])
        for j, part in enumerate(parts):
            total = total + jnp.where(chunk_mask(j, part.shape[1]), part, 0.0)
        total = jnp.concatenate([total] + tails, axis=0)
        return jnp.dot(join, total, precision=lax.Precision.HIGHEST, preferred_element_type=F32)

    def spread(value, j):
        return jnp.where(chunk_mask(j, value.shape[1]), value, 0.0).astype(BF16)

    def groups(body):
        if n == GROUP:
            body(0)
        else:
            pl.loop(0, n // GROUP)(lambda b: body(b * GROUP))

    def block(ref, u, b):
        return ref[u, pl.ds(b, GROUP)].reshape(rows, chunk)

    def tails_of(x):
        return [x[:, c * tail:(c + 1) * tail] for c in range(CAP)]

    def gate_ups(x):
        return joined(
            [mm(x, wgu[j]) for j in range(FOLD)], [mm(part, wgu_tail[...]) for part in tails_of(x)])

    def answer_with(total, last):
        last = last.astype(BF16)
        whole = with_tails(total, [mm(place, last) for place in to_tail])
        return whole.astype(BF16).reshape(GROUP, BLOCK, chunk)

    def forward(b):
        gate, up, sigma = activations(gate_ups(block(rcv, 0, b)))
        hidden = gate * sigma * up
        total = sum(mm(spread(hidden, j), wd[j]) for j in range(FOLD))
        ret_snd[0, pl.ds(b, GROUP)] = answer_with(total, mm(hidden.astype(BF16), wd_tail[...]))

    def backward(b):
        y = block(rcv, 2, b)
        gate, up, sigma = activations(gate_ups(block(rcv, 1, b)))
        d_hidden = joined(
            [mm_nt(y, wd[j]) for j in range(FOLD)], [mm_nt(part, wd_tail[...]) for part in tails_of(y)])
        both = jnp.concatenate(cotangents(d_hidden, gate, up, sigma), axis=1)
        total = sum(mm_nt(spread(both.astype(F32), j), wgu[j]) for j in range(FOLD))
        ret_snd[1, pl.ds(b, GROUP)] = answer_with(total, mm_nt(both, wgu_tail[...]))

    for u in (1, 2):
        for k in order:
            send_copy(u, k).wait_recv()
        own_copy(u).wait()
    groups(backward)
    for k in order:
        ret_copy(1, k).start()
    own_ret(1).start()

    for k in order:
        send_copy(0, k).wait_recv()
    own_copy(0).wait()
    groups(forward)
    for k in order:
        ret_copy(0, k).start()
    own_ret(0).start()

    for k in range(1, ne):
        rows_copy(k).wait_recv()
        factor_copy(k).wait_recv()
    own_rows.wait()
    own_factors.wait()
    all_rows = rcv3[:, 0:count3, :].reshape(ne * count3, span)
    all_cots = rcv3[:, count3:2 * count3, :].reshape(ne * count3, span)
    factors = fac_rcv[...].reshape(ne * count3, 3 * h)
    pair = mm_tn(all_rows, factors[:, 0:2 * h]).astype(BF16)
    grads_buf[0] = pair[:, 0:h]
    grads_buf[1] = pair[:, h:2 * h]
    grads_buf[2] = mm_tn(all_cots, factors[:, 2 * h:3 * h]).astype(BF16)

    stores = [
        pltpu.make_async_copy(source, target, out_sem.at[i])
        for i, (source, target) in enumerate(((grads_buf, grads), (out1_buf, out1), (dx2_buf, dx2)))]
    stores[0].start()

    back = n * BLOCK
    first, second, masks = slots(rt1[...], back, slices)
    weight = jnp.where(first, gt1[0:1, :], 0.0) + jnp.where(second, gt1[1:2, :], 0.0)
    pieces = []
    for mask in masks:
        rest = jnp.where(mask, weight, 0.0)
        split = []
        for _ in range(3):
            split.append(rest.astype(BF16))
            rest = rest - split[-1].astype(F32)
        pieces.append(jnp.concatenate([turned(piece) for piece in split], axis=0))
    first, second, masks = slots(rt2[...], back, slices)
    picked = [turned(ones((first | second) & mask)) for mask in masks]

    def unpacked(weights, answer):
        yield from ((at, size, mm(weights[j], answer)) for j, (at, size) in enumerate(spans))
        yield cut, tail, sum(mm(weights[FOLD + c], part) for c, part in enumerate(tails_of(answer)))

    for k in order:
        ret_copy(1, k).wait_recv()
    own_ret(1).wait()
    for at, size, result in unpacked(picked, ret_rcv[1].reshape(back, chunk)):
        dx2_buf[:, at:at + size] = result.astype(BF16)
    stores[2].start()

    for k in order:
        ret_copy(0, k).wait_recv()
    own_ret(0).wait()
    for at, size, result in unpacked(pieces, ret_rcv[0].reshape(back, chunk)):
        out1_buf[:, at:at + size] = (
            result[0:BLOCK] + result[BLOCK:2 * BLOCK] + result[2 * BLOCK:3 * BLOCK]).astype(BF16)
    stores[1].start()

    for k in order:
        for u in range(3):
            send_copy(u, k).wait_send()
        for u in range(2):
            ret_copy(u, k).wait_send()
    for k in range(1, ne):
        rows_copy(k).wait_send()
        factor_copy(k).wait_send()
    for copy in stores:
        copy.wait()


def store(a, b, c, a_out, b_out, c_out, a_buf, b_buf, c_buf, in_sem, out_sem):
    triples = [(c.at[i], c_buf.at[i], c_out.at[i]) for i in range(c.shape[0])]
    triples += [(a, a_buf, a_out), (b, b_buf, b_out)]
    loads = [pltpu.make_async_copy(t[0], t[1], in_sem.at[i]) for i, t in enumerate(triples)]
    saves = [pltpu.make_async_copy(t[1], t[2], out_sem.at[i]) for i, t in enumerate(triples)]
    for load in loads:
        load.start()
    for load, save in zip(loads, saves):
        load.wait()
        save.start()
    for save in saves:
        save.wait()


def shards(*args):
    args = [arg.T if i in (1, 2, 4, 5) else arg for i, arg in enumerate(args)]
    n = lax.axis_size("expert")
    ne = lax.axis_size("edata")
    tokens, depth = args[0].shape
    count3 = args[7].shape[0]
    h = args[9].shape[1]
    span = depth // ne
    chunk = depth // (FOLD * 128) * 128
    tail = depth - FOLD * chunk
    hbm = pl.BlockSpec(memory_space=pl.ANY)
    results = (
            jax.ShapeDtypeStruct((tokens, depth), BF16),
            jax.ShapeDtypeStruct((tokens, depth), BF16),
            jax.ShapeDtypeStruct((3, span, h), BF16),
    )
    landed = pl.pallas_call(
        functools.partial(kernel, n, ne),
        out_shape=results,
        in_specs=[hbm] * 12,
        out_specs=(hbm,) * 3,
        scratch_shapes=[pltpu.VMEM(arg.shape, arg.dtype) for arg in args[:9]] + [
            pltpu.SemaphoreType.DMA((9,)),
            pltpu.VMEM((tokens, depth), BF16),
            pltpu.VMEM((tokens, depth), BF16),
            pltpu.VMEM((3, span, h), BF16),
            pltpu.SemaphoreType.DMA((3,)),
            pltpu.VMEM((tail, 2 * h), BF16),
            pltpu.VMEM((h, tail), BF16),
            pltpu.VMEM((FOLD, chunk, 2 * h), BF16),
            pltpu.VMEM((FOLD, h, chunk), BF16),
            pltpu.VMEM((3, EXPERTS, BLOCK, chunk), BF16),
            pltpu.VMEM((3, n, BLOCK, chunk), BF16),
            pltpu.VMEM((2, n, BLOCK, chunk), BF16),
            pltpu.VMEM((2, n, BLOCK, chunk), BF16),
            pltpu.VMEM((ne, 2 * count3, span), BF16),
            pltpu.VMEM((ne, 2 * count3, span), BF16),
            pltpu.VMEM((count3, 3 * h), BF16),
            pltpu.VMEM((ne, count3, 3 * h), BF16),
            pltpu.SemaphoreType.DMA((3 * FOLD + 3,)),
            pltpu.SemaphoreType.DMA((7,)),
            pltpu.SemaphoreType.DMA((3, n)),
            pltpu.SemaphoreType.DMA((3, n)),
            pltpu.SemaphoreType.DMA((2, n)),
            pltpu.SemaphoreType.DMA((2, n)),
            pltpu.SemaphoreType.DMA((2, ne)),
            pltpu.SemaphoreType.DMA((2, ne)),
        ],
        compiler_params=pltpu.CompilerParams(
            collective_id=0, has_side_effects=True, vmem_limit_bytes=62 * 2**20),
    )(*args)
    out_one, dx_two, grads = pl.pallas_call(
        store,
        out_shape=results,
        in_specs=[hbm] * 3,
        out_specs=(hbm,) * 3,
        scratch_shapes=[pltpu.VMEM(result.shape, result.dtype) for result in results]
        + [pltpu.SemaphoreType.DMA((5,)), pltpu.SemaphoreType.DMA((5,))],
        compiler_params=pltpu.CompilerParams(vmem_limit_bytes=62 * 2**20),
    )(*landed)
    return out_one, dx_two, jnp.transpose(grads, (1, 0, 2))


def solution(mesh):
    both = P(("edata", "expert"), None)
    return jax.shard_map(
        shards,
        mesh=mesh,
        in_specs=(both,) * 9 + (P(None, "expert"), P(None, "expert"), P("expert", None)),
        out_specs=(both, both, P("edata", None, "expert")),
        check_vma=False,
    )
```
